128 devices in a mesh: slab: 16 (over y, x), view: 8 (over z, core).
Axes of the slice: x: 4, y: 4, z: 4, core: 2. Of those that a mesh axis runs over, the one named last changes fastest.
Arguments:
- object_field: float32 [2, 128, 1024, 1024], P(None, 'view', 'slab'), may hold values from -0.8 to 0.8
- probe: float32 [2, 256, 256], replicated, may hold values from -6 to 6
- amplitude: float32 [4096, 256, 256], P(('slab', 'view')), may hold values from 0.1 to 3
- offsets: int32 [4096, 2], P(('slab', 'view')), may hold values from 0 to 1023, as said below
Outputs:
- object_new: float32 [2, 128, 1024, 1024], P(None, 'view', 'slab')
- probe_step: float32 [2, 256, 256], replicated
The draws below stay inside these ranges and needn't reach their ends.
Inputs may be any that keep to these rules, and one draw needn't show every extreme that they name: `offsets`: A position handled by the device at slab index s has its row offset in s * 64 to (s + 1) * 64 - 1 and its column offset in 0 to 768; on every device the first position lies at the slab's first row and column 0 and the second at the slab's last row and column 768.
All inputs are finite; a program needn't handle non-finite values.
Results may differ from the reference program's by a relative error of at most 0.0029.
Values may be sent and summed in bfloat16 or wider, within the bound.
No kernel may reach another device: no remote copies, remote signals or barrier semaphores. Data moves between devices by JAX's collectives and lax.ppermute only.
A program may use at most 128 MiB of HBM per device.

```python
import math
import jax
import jax.numpy as jnp
from jax import lax

FRAME = 256
ROWS_SLAB = 64
NYO = 1024
POS_DEV = 32
NXO = 1024
DEPTH = 128
POSITIONS = 4096
N_VIEW = 8


def draw_offsets(key, part):
    key = jax.random.fold_in(key, 11)
    key_rows, key_cols = jax.random.split(key)
    index = jnp.arange(POSITIONS, dtype=jnp.int32)
    within = index % POS_DEV
    slab_index = index // POS_DEV // N_VIEW
    row_part = jax.random.randint(key_rows, (POSITIONS,), 0, ROWS_SLAB, dtype=jnp.int32)
    row_part = jnp.where(within == 0, 0, jnp.where(within == 1, ROWS_SLAB - 1, row_part))
    column = jax.random.randint(key_cols, (POSITIONS,), 0, NYO - FRAME + 1, dtype=jnp.int32)
    column = jnp.where(within == 0, 0, jnp.where(within == 1, NYO - FRAME, column))
    return jnp.stack([slab_index * ROWS_SLAB + row_part, column], axis=1).astype(jnp.int32)


def level_of(stream_key, shape, cuts, low, high):
    def one(position, shards_of):
        draws = jax.random.uniform(jax.random.fold_in(jax.random.fold_in(stream_key, 6), position), (shards_of,), jnp.float32, low / len(cuts), high / len(cuts))
        return jnp.repeat(jnp.exp(draws), shape[position] // shards_of).reshape((-1,) + (1,) * (len(shape) - position - 1))

    level = one(*cuts[0])
    for cut in cuts[1:]:
        level = level * one(*cut)
    return level


def gaussian(stream_key, shape, width, limit, shards=(), kind=jnp.bfloat16):
    entries = width * jax.random.normal(stream_key, shape, jnp.float32)
    if shards:
        entries = entries * level_of(stream_key, shape, shards, -0.22, 0.18)
    return jnp.clip(entries, -limit, limit).astype(kind)


def setup_inputs(seed: int = 0) -> dict:
    key_of = jax.random.split(jax.random.key(seed), 5)
    object_field = gaussian(key_of[0], (2, DEPTH, NXO, NYO), 0.1, 0.8, ((1, 8), (2, 16)), jnp.float32)
    probe = gaussian(key_of[1], (2, FRAME, FRAME), 1.0, 6.0, (), jnp.float32)
    amplitude = jnp.clip(jnp.exp(math.log(3.0) - 3.4011974 * jax.random.uniform(key_of[2], (POSITIONS, FRAME, FRAME), jnp.float32) ** level_of(key_of[2], (POSITIONS, FRAME, FRAME), ((0, 128),), -0.2, 0.2)), 0.1, 3.0)
    offsets = draw_offsets(jax.random.fold_in(key_of[4], 71), 0)
    return dict(object_field=object_field, probe=probe, amplitude=amplitude, offsets=offsets)


def dft_tables(order):
    index = jnp.arange(order, dtype=jnp.int32)
    product = index[:, None] * index[None, :] % order
    angle = product.astype(jnp.float32) * (-2.0 * math.pi / order)
    factor = 1.0 / math.sqrt(order)
    return (jnp.cos(angle) * factor, jnp.sin(angle) * factor)

def real_dot(left, right):
    return jnp.dot(left, right, precision=lax.Precision.HIGHEST, preferred_element_type=jnp.float32)

def complex_dot(left_re, left_im, right_re, right_im):
    out_re = real_dot(left_re, right_re) - real_dot(left_im, right_im)
    out_im = real_dot(left_re, right_im) + real_dot(left_im, right_re)
    return (out_re, out_im)

def exit_update(patch, probe, amplitude, cosines, sines):
    patch_re, patch_im = (patch[0], patch[1])
    probe_re, probe_im = (probe[0], probe[1])
    exit_re = probe_re * patch_re - probe_im * patch_im
    exit_im = probe_re * patch_im + probe_im * patch_re
    half_re, half_im = complex_dot(cosines, sines, exit_re, exit_im)
    far_re, far_im = complex_dot(half_re, half_im, cosines, sines)
    factor = amplitude / jnp.sqrt(far_re * far_re + far_im * far_im + 0.25)
    fixed_re, fixed_im = (far_re * factor, far_im * factor)
    back_re, back_im = complex_dot(cosines, -sines, fixed_re, fixed_im)
    new_re, new_im = complex_dot(back_re, back_im, cosines, -sines)
    diff_re, diff_im = (new_re - exit_re, new_im - exit_im)
    object_term = jnp.stack([probe_re * diff_re + probe_im * diff_im, probe_re * diff_im - probe_im * diff_re])
    probe_term = jnp.stack([patch_re * diff_re + patch_im * diff_im, patch_re * diff_im - patch_im * diff_re])
    weight = patch_re * patch_re + patch_im * patch_im
    return (object_term, probe_term, weight)

def reference(object_field, probe, amplitude, offsets):
    cosines, sines = dft_tables(FRAME)
    zero_index = jnp.zeros((), jnp.int32)

    def add_layer(total, layer_id):
        layer = lax.dynamic_index_in_dim(object_field, layer_id, 1, keepdims=False)
        padded = jnp.pad(layer, ((0, 0), (0, 0), (DEPTH, 0)))
        return (total + lax.dynamic_slice_in_dim(padded, DEPTH - layer_id, NYO, 2), None)
    layer_ids = jnp.arange(DEPTH, dtype=jnp.int32)
    projected, _ = lax.scan(add_layer, jnp.zeros((2, NXO, NYO), jnp.float32), layer_ids)
    projected = projected.astype(jnp.bfloat16)
    padded_field = jnp.pad(projected, ((0, 0), (0, FRAME), (0, 0)))

    def visit(carry, item):
        update, numer, denom = carry
        corner, measured = item
        starts = (zero_index, corner[0], corner[1])
        patch = lax.dynamic_slice(padded_field, starts, (2, FRAME, FRAME)).astype(jnp.float32)
        object_term, probe_term, weight = exit_update(patch, probe, measured, cosines, sines)
        current = lax.dynamic_slice(update, starts, (2, FRAME, FRAME))
        update = lax.dynamic_update_slice(update, current + object_term, starts)
        return ((update, numer + probe_term, denom + weight), None)
    start = (jnp.zeros((2, NXO + FRAME, NYO), jnp.float32), jnp.zeros((2, FRAME, FRAME), jnp.float32), jnp.zeros((FRAME, FRAME), jnp.float32))
    (update, numer, denom), _ = lax.scan(visit, start, (offsets, amplitude))
    update = jnp.pad(update[:, :NXO], ((0, 0), (0, 0), (0, DEPTH)))
    peak = jnp.max(probe[0] * probe[0] + probe[1] * probe[1]) + 1e-06

    def spread(layer_id):
        return lax.dynamic_slice_in_dim(update, layer_id, NYO, 2)
    back = lax.map(spread, layer_ids)
    object_new = object_field + 0.5 * jnp.moveaxis(back, 0, 1) / peak
    probe_step = numer / denom[None]
    return (object_new, probe_step)
```

```python
import functools
import math

import jax
import jax.numpy as jnp
import ml_dtypes
import numpy as np
from jax import lax
from jax.experimental import pallas as pl
from jax.experimental.pallas import tpu as pltpu
from jax.sharding import PartitionSpec as P

F32 = jnp.float32
BF16 = jnp.bfloat16
FRAME = 256
LANES = 128
SLAB = 64
VIEWS = 8
ROWS = SLAB // VIEWS
COLUMNS = 1024
TILES = COLUMNS // LANES
BLOCKS = 5
BAND = BLOCKS * SLAB
PER_STEP = 4
VMEM = pl.BlockSpec(memory_space=pltpu.VMEM)
SMEM = pl.BlockSpec(memory_space=pltpu.SMEM)


def dft_blocks(order):
    index = np.arange(order, dtype=np.int32)
    product = index[:, None] * index[None, :] % order
    angle = product.astype(np.float32) * np.float32(-2.0 * math.pi / order)
    factor = np.float32(1.0 / math.sqrt(order))
    c, s = np.cos(angle) * factor, np.sin(angle) * factor
    fore = np.block([[c, -s], [s, c]]).astype(ml_dtypes.bfloat16)
    back = np.block([[c, s], [-s, c]]).astype(ml_dtypes.bfloat16)
    return fore, back


def shifted(value, steps, left):
    lane = lax.broadcasted_iota(jnp.int32, value.shape, 1)
    if left:
        return jnp.where(lane < COLUMNS - steps, pltpu.roll(value, (COLUMNS - steps) % COLUMNS, 1), 0.0)
    return jnp.where(lane >= steps, pltpu.roll(value, steps, 1), 0.0)


def project_kernel(first_ref, field_ref, out_ref):
    layers = field_ref.shape[1]

    def layer(k):
        return jnp.concatenate([field_ref[0, k], field_ref[1, k]], 0)

    total = layer(layers - 1)
    for k in reversed(range(layers - 1)):
        total = shifted(total, 1, False) + layer(k)
    out_ref[0] = shifted(total, first_ref[0], False)


def project(first, field):
    layers = field.shape[1]
    return pl.pallas_call(
        project_kernel,
        grid=(VIEWS,),
        in_specs=[SMEM, pl.BlockSpec((2, layers, ROWS, COLUMNS), lambda i: (0, 0, i, 0))],
        out_specs=pl.BlockSpec((1, 2 * ROWS, COLUMNS), lambda i: (i, 0, 0)),
        out_shape=jax.ShapeDtypeStruct((VIEWS, 2 * ROWS, COLUMNS), F32),
        compiler_params=pltpu.CompilerParams(vmem_limit_bytes=32 << 20),
    )(first, field)


def spread_kernel(first_ref, update_ref, field_ref, out_ref):
    layers = field_ref.shape[1]
    update = shifted(update_ref[0].astype(F32), first_ref[0], True)
    for k in range(layers):
        for part in range(2):
            out_ref[part, k] = field_ref[part, k] + update[part * ROWS : (part + 1) * ROWS]
        if k < layers - 1:
            update = shifted(update, 1, True)


def spread(first, update, field):
    layers = field.shape[1]
    block = pl.BlockSpec((2, layers, ROWS, COLUMNS), lambda i: (0, 0, i, 0))
    return pl.pallas_call(
        spread_kernel,
        grid=(VIEWS,),
        in_specs=[SMEM, pl.BlockSpec((1, 2 * ROWS, COLUMNS), lambda i: (i, 0, 0)), block],
        out_specs=block,
        out_shape=jax.ShapeDtypeStruct(field.shape, F32),
        compiler_params=pltpu.CompilerParams(vmem_limit_bytes=32 << 20),
    )(first, update, field)


def dot(left, right):
    return jnp.dot(left, right, preferred_element_type=F32)


def visit_kernel(off_ref, b0, b1, b2, b3, b4, probe_ref, fore_ref, back_ref, amp_ref, out_ref, band, upd, num):
    step = pl.program_id(0)

    @pl.when(step == 0)
    def _():
        for b, ref in enumerate((b0, b1, b2, b3, b4)):
            for v in range(VIEWS):
                x = ref[v].astype(F32)
                first = b * SLAB + v * ROWS
                for part in range(2):
                    for t in range(TILES):
                        band[part, t, first : first + ROWS, :] = x[part * ROWS : (part + 1) * ROWS, t * LANES : (t + 1) * LANES]
        upd[...] = jnp.zeros_like(upd)
        num[...] = jnp.zeros_like(num)

    lane = lax.broadcasted_iota(jnp.int32, (FRAME, LANES), 1)

    def corner(j):
        p = step * PER_STEP + j
        r, c = off_ref[p, 0], off_ref[p, 1]
        q, m = c // LANES, c % LANES
        return r, (q, q + 1, jnp.minimum(q + 2, TILES - 1)), m

    def patch_of(part, r, q, m):
        turn = (LANES - m) % LANES
        tiles = [pltpu.roll(band[part, t, pl.ds(r, FRAME), :], turn, 1) for t in q]
        keep = lane < LANES - m
        return jnp.concatenate([jnp.where(keep, tiles[0], tiles[1]), jnp.where(keep, tiles[1], tiles[2])], 1)

    def add_to(part, value, r, q, m):
        left = pltpu.roll(value[:, :LANES], m, 1)
        right = pltpu.roll(value[:, LANES:], m, 1)
        keep = lane >= m
        terms = [jnp.where(keep, left, 0.0), jnp.where(keep, right, left), jnp.where(keep, 0.0, right)]
        for t, x in zip(q, terms):
            upd[part, t, pl.ds(r, FRAME), :] += x

    pr, pi = probe_ref[0], probe_ref[1]
    corners = [corner(j) for j in range(PER_STEP)]
    stage = []
    for r, q, m in corners:
        a, b = patch_of(0, r, q, m), patch_of(1, r, q, m)
        stage.append((a, b, pr * a - pi * b, pr * b + pi * a))
    half = [dot(fore_ref[...], jnp.concatenate([er, ei], 0).astype(BF16)) for _, _, er, ei in stage]
    half = [jnp.concatenate([h[:FRAME], h[FRAME:]], 1).astype(BF16) for h in half]
    far = [dot(h, back_ref[...]) for h in half]
    fixed = []
    for j, f in enumerate(far):
        fr, fi = f[:, :FRAME], f[:, FRAME:]
        factor = amp_ref[j] * lax.rsqrt(fr * fr + fi * fi + 0.25)
        fixed.append(jnp.concatenate([fr * factor, fi * factor], 1).astype(BF16))
    back = [dot(g, fore_ref[...]) for g in fixed]
    back = [jnp.concatenate([h[:, :FRAME], h[:, FRAME:]], 0).astype(BF16) for h in back]
    new = [dot(back_ref[...], h) for h in back]
    for (r, q, m), (a, b, er, ei), n in zip(corners, stage, new):
        dr, di = n[:FRAME] - er, n[FRAME:] - ei
        add_to(0, pr * dr + pi * di, r, q, m)
        add_to(1, pr * di - pi * dr, r, q, m)
        num[0] += a * dr + b * di
        num[1] += a * di - b * dr
        num[2] += a * a + b * b

    @pl.when(step == pl.num_programs(0) - 1)
    def _():
        peak = jnp.max(pr * pr + pi * pi) + 1e-06
        scale = 0.5 / jnp.full((2 * ROWS, COLUMNS), peak, F32)
        for v in range(VIEWS):
            for b in range(BLOCKS):
                rows = slice(b * SLAB + v * ROWS, b * SLAB + (v + 1) * ROWS)
                x = [jnp.concatenate([upd[part, t, rows, :] for t in range(TILES)], 1) for part in range(2)]
                out_ref[v, b * 2 * ROWS : (b + 1) * 2 * ROWS, :] = (jnp.concatenate(x, 0) * scale).astype(BF16)
            first = v * (FRAME // VIEWS)
            planes = [
                jnp.concatenate([num[k, first + g * ROWS : first + (g + 1) * ROWS, :] for g in range(4)], 1) for k in range(3)
            ]
            out_ref[v, 80:112, :] = jnp.concatenate(planes + [jnp.zeros_like(planes[0])], 0).astype(BF16)


def visit_all(corners, bands, probe, amplitude):
    count = amplitude.shape[0]
    fore, back = dft_blocks(FRAME)
    amp_spec = pl.BlockSpec((PER_STEP, FRAME, FRAME), lambda i: (i, 0, 0))
    return pl.pallas_call(
        visit_kernel,
        grid=(count // PER_STEP,),
        in_specs=[SMEM] + [VMEM] * 8 + [amp_spec],
        out_specs=VMEM,
        out_shape=jax.ShapeDtypeStruct((VIEWS, 112, COLUMNS), BF16),
        scratch_shapes=[
            pltpu.VMEM((2, TILES, BAND, LANES), F32),
            pltpu.VMEM((2, TILES, BAND, LANES), F32),
            pltpu.VMEM((3, FRAME, FRAME), F32),
        ],
        compiler_params=pltpu.CompilerParams(vmem_limit_bytes=48 << 20),
    )(corners, *bands, probe, fore, back, amplitude)


def passed_along(value, steps):
    count = lax.axis_size("slab")
    first, last = (max(0, -steps), min(count, count - steps))
    return lax.ppermute(value, "slab", [(source, source + steps) for source in range(first, last)])


def on_device(object_field, probe, amplitude, offsets):
    layers = object_field.shape[1]
    first = (lax.axis_index("view") * layers).astype(jnp.int32).reshape(1)
    corners = offsets - jnp.stack([lax.axis_index("slab") * SLAB, 0]).astype(jnp.int32)
    partial = project(first, object_field)
    got = lax.all_to_all(partial, "view", 0, 0, tiled=True)
    piece = jnp.sum(got, axis=0).astype(BF16)
    band = lax.all_gather(piece, "view", axis=0)
    bands = [band] + [passed_along(band, -k) for k in range(1, BLOCKS)]
    terms = visit_all(corners, bands, probe, amplitude)
    got = lax.all_to_all(terms, "view", 0, 0, tiled=True)
    sums = jnp.sum(got.astype(F32), axis=0)
    update = sums[: 2 * ROWS]
    for k in range(1, BLOCKS):
        update = update + passed_along(sums[k * 2 * ROWS : (k + 1) * 2 * ROWS], k)
    totals = sums[80:104]
    for k in (1, 2, 4, 8):
        totals = totals + lax.ppermute(totals, "slab", [(i, i ^ k) for i in range(lax.axis_size("slab"))])
    ratio = (totals[:16].reshape(2, ROWS, 4, FRAME) / totals[16:].reshape(1, ROWS, 4, FRAME)).reshape(16, COLUMNS)
    whole = lax.all_gather(jnp.concatenate([update.astype(BF16), ratio.astype(BF16)], 0), "view", axis=0)
    object_new = spread(first, whole[:, :16], object_field)
    ratios = whole[:, 16:].astype(F32).reshape(VIEWS, 2, ROWS, 4, FRAME)
    probe_step = ratios.transpose(1, 0, 3, 2, 4).reshape(2, FRAME, FRAME)
    return object_new, probe_step


def solution(mesh):
    return jax.shard_map(
        on_device,
        mesh=mesh,
        in_specs=(P(None, "view", "slab", None), P(), P(("slab", "view"), None, None), P(("slab", "view"), None)),
        out_specs=(P(None, "view", "slab", None), P()),
        check_vma=False,
    )
```

```python
import functools
import math

import jax
import jax.numpy as jnp
import ml_dtypes
import numpy as np
from jax import lax
from jax.experimental import pallas as pl
from jax.experimental.pallas import tpu as pltpu
from jax.sharding import PartitionSpec as P

F32 = jnp.float32
BF16 = jnp.bfloat16
FRAME = 256
LANES = 128
SLAB = 64
VIEWS = 8
ROWS = SLAB // VIEWS
COLUMNS = 1024
TILES = COLUMNS // LANES
BLOCKS = 5
BAND = BLOCKS * SLAB
PER_STEP = 4
SUMS = BLOCKS * SLAB + 4 * 4 * ROWS
VMEM = pl.BlockSpec(memory_space=pltpu.VMEM)
SMEM = pl.BlockSpec(memory_space=pltpu.SMEM)


def dft_blocks(order):
    index = np.arange(order, dtype=np.int32)
    product = index[:, None] * index[None, :] % order
    angle = product.astype(np.float32) * np.float32(-2.0 * math.pi / order)
    factor = np.float32(1.0 / math.sqrt(order))
    c, s = np.cos(angle) * factor, np.sin(angle) * factor
    fore = np.block([[c, -s], [s, c]]).astype(ml_dtypes.bfloat16)
    back = np.block([[c, s], [-s, c]]).astype(ml_dtypes.bfloat16)
    return fore, back


def tiles_of(value):
    return [value[:, t * LANES : (t + 1) * LANES] for t in range(TILES)]


def to_right(tiles, steps):
    lane = lax.broadcasted_iota(jnp.int32, tiles[0].shape, 1)
    turned = [pltpu.roll(x, steps, 1) for x in tiles]
    return [jnp.where(lane >= steps, x, before) for x, before in zip(turned, [jnp.zeros_like(tiles[0])] + turned)]


def to_left(tiles, steps):
    lane = lax.broadcasted_iota(jnp.int32, tiles[0].shape, 1)
    turned = [pltpu.roll(x, (LANES - steps) % LANES, 1) for x in tiles]
    return [jnp.where(lane < LANES - steps, x, after) for x, after in zip(turned, turned[1:] + [jnp.zeros_like(tiles[0])])]


def chunk_at(place, half, j):
    return 4 * ((place[1] + half) % 2) + (place[0] + 4 - j) % 4


def project_kernel(place, field_ref, out_ref):
    layers = field_ref.shape[1]
    values = [tiles_of(jnp.concatenate([field_ref[0, k], field_ref[1, k]], 0)) for k in range(layers)]
    steps = 1
    while len(values) > 1:
        moved = [to_right(x, steps) for x in values[1::2]]
        values = [[a + b for a, b in zip(x, y)] for x, y in zip(values[0::2], moved)]
        steps *= 2
    for t, x in enumerate(to_right(values[0], place[2])):
        out_ref[0, :, t * LANES : (t + 1) * LANES] = x


def project(place, field, half):
    layers = field.shape[1]
    return pl.pallas_call(
        project_kernel,
        grid_spec=pltpu.PrefetchScalarGridSpec(
            num_scalar_prefetch=1,
            grid=(4,),
            in_specs=[pl.BlockSpec((2, layers, ROWS, COLUMNS), lambda i, place: (0, 0, chunk_at(place, half, 4 - i), 0))],
            out_specs=pl.BlockSpec((1, 2 * ROWS, COLUMNS), lambda i, place: (i, 0, 0)),
        ),
        out_shape=jax.ShapeDtypeStruct((4, 2 * ROWS, COLUMNS), F32),
        compiler_params=pltpu.CompilerParams(vmem_limit_bytes=60 << 20),
        cost_estimate=pl.CostEstimate(flops=layers * 4 * 16 * 1024 * 6, bytes_accessed=(4 << 20) + (256 << 10), transcendentals=0),
    )(place, field)


def spread_kernel(place, mine_ref, theirs_ref, field_ref, out_ref):
    layers = field_ref.shape[1]
    half, j = pl.program_id(0), pl.program_id(1)
    rows = pl.ds(pl.multiple_of(j * 2 * ROWS, 2 * ROWS), 2 * ROWS)
    update = jnp.where(half == 0, mine_ref[rows, :].astype(F32), theirs_ref[rows, :].astype(F32))
    base = to_left(tiles_of(update), place[2])
    for k in range(layers):
        for t, x in enumerate(to_left(base, k) if k else base):
            for part in range(2):
                columns = slice(t * LANES, (t + 1) * LANES)
                out_ref[part, k, :, columns] = field_ref[part, k, :, columns] + x[part * ROWS : (part + 1) * ROWS]


def spread(place, mine, theirs, field):
    layers = field.shape[1]
    block = pl.BlockSpec((2, layers, ROWS, COLUMNS), lambda i, j, place: (0, 0, chunk_at(place, i, j), 0))
    return pl.pallas_call(
        spread_kernel,
        grid_spec=pltpu.PrefetchScalarGridSpec(
            num_scalar_prefetch=1, grid=(2, 4), in_specs=[VMEM, VMEM, block], out_specs=block
        ),
        out_shape=jax.ShapeDtypeStruct(field.shape, F32),
        compiler_params=pltpu.CompilerParams(vmem_limit_bytes=32 << 20),
        cost_estimate=pl.CostEstimate(flops=layers * 8 * 16 * 1024 * 4, bytes_accessed=16 << 20, transcendentals=0),
    )(place, mine, theirs, field)


def join_kernel(place, mine_ref, theirs_ref, out_ref):
    for half, ref in enumerate((mine_ref, theirs_ref)):
        for j in range(4):
            first = chunk_at(place, half, j) * (FRAME // VIEWS)
            for part in range(2):
                x = ref[j * 2 * ROWS : (j + 1) * 2 * ROWS, :][part * ROWS : (part + 1) * ROWS]
                for g in range(4):
                    rows = pl.ds(pl.multiple_of(first + g * ROWS, ROWS), ROWS)
                    out_ref[part, rows, :] = x[:, g * FRAME : (g + 1) * FRAME].astype(F32)


def join(place, mine, theirs):
    return pl.pallas_call(
        join_kernel,
        in_specs=[SMEM, VMEM, VMEM],
        out_specs=VMEM,
        out_shape=jax.ShapeDtypeStruct((2, FRAME, FRAME), F32),
        cost_estimate=pl.CostEstimate(flops=1000, bytes_accessed=1 << 20, transcendentals=0),
    )(place, mine, theirs)


def dot(left, right):
    return jnp.dot(left, right, preferred_element_type=F32)


def visit_kernel(place, off_ref, *refs):
    bands, (probe_ref, fore_ref, back_ref, amp_ref, mine_ref, theirs_ref, band, upd, num) = refs[:10], refs[10:]
    step = pl.program_id(0)

    @pl.when(step == 0)
    def _():
        for i, ref in enumerate(bands):
            for j in range(4):
                x = ref[j * 2 * ROWS : (j + 1) * 2 * ROWS, :].astype(F32)
                first = pl.multiple_of(i % BLOCKS * SLAB + chunk_at(place, i // BLOCKS, j) * ROWS, ROWS)
                for part in range(2):
                    for t in range(TILES):
                        band[part, t, pl.ds(first, ROWS), :] = x[part * ROWS : (part + 1) * ROWS, t * LANES : (t + 1) * LANES]
        upd[...] = jnp.zeros_like(upd)
        num[...] = jnp.zeros_like(num)

    lane = lax.broadcasted_iota(jnp.int32, (FRAME, LANES), 1)

    def corner(j):
        p = step * PER_STEP + j
        r, c = off_ref[p, 0], off_ref[p, 1]
        q, m = c // LANES, c % LANES
        return r, (q, q + 1, jnp.minimum(q + 2, TILES - 1)), m

    def patch_of(part, r, q, m):
        turn = (LANES - m) % LANES
        tiles = [pltpu.roll(band[part, t, pl.ds(r, FRAME), :], turn, 1) for t in q]
        keep = lane < LANES - m
        return jnp.concatenate([jnp.where(keep, tiles[0], tiles[1]), jnp.where(keep, tiles[1], tiles[2])], 1)

    def add_to(part, value, r, q, m):
        left = pltpu.roll(value[:, :LANES], m, 1)
        right = pltpu.roll(value[:, LANES:], m, 1)
        keep = lane >= m
        terms = [jnp.where(keep, left, 0.0), jnp.where(keep, right, left), jnp.where(keep, 0.0, right)]
        for t, x in zip(q, terms):
            upd[part, t, pl.ds(r, FRAME), :] += x

    pr, pi = probe_ref[0], probe_ref[1]
    corners = [corner(j) for j in range(PER_STEP)]
    stage = []
    for r, q, m in corners:
        a, b = patch_of(0, r, q, m), patch_of(1, r, q, m)
        stage.append((a, b, pr * a - pi * b, pr * b + pi * a))
    half = [dot(fore_ref[...], jnp.concatenate([er, ei], 0).astype(BF16)) for _, _, er, ei in stage]
    half = [jnp.concatenate([h[:FRAME], h[FRAME:]], 1).astype(BF16) for h in half]
    far = [dot(h, back_ref[...]) for h in half]
    fixed = []
    for j, f in enumerate(far):
        fr, fi = f[:, :FRAME], f[:, FRAME:]
        factor = amp_ref[j] * lax.rsqrt(fr * fr + fi * fi + 0.25)
        fixed.append(jnp.concatenate([fr * factor, fi * factor], 1).astype(BF16))
    back = [dot(g, fore_ref[...]) for g in fixed]
    back = [jnp.concatenate([h[:, :FRAME], h[:, FRAME:]], 0).astype(BF16) for h in back]
    new = [dot(back_ref[...], h) for h in back]
    for (r, q, m), (a, b, er, ei), n in zip(corners, stage, new):
        dr, di = n[:FRAME] - er, n[FRAME:] - ei
        add_to(0, pr * dr + pi * di, r, q, m)
        add_to(1, pr * di - pi * dr, r, q, m)
        num[0] += a * dr + b * di
        num[1] += a * di - b * dr
        num[2] += a * a + b * b

    @pl.when(step == pl.num_programs(0) - 1)
    def _():
        peak = jnp.max(pr * pr + pi * pi) + 1e-06
        scale = 0.5 / jnp.full((2 * ROWS, COLUMNS), peak, F32)
        for half, ref in enumerate((mine_ref, theirs_ref)):
            for e in range(4):
                chunk = chunk_at(place, half, 4 - e)
                for b in range(BLOCKS):
                    rows = pl.ds(pl.multiple_of(b * SLAB + chunk * ROWS, ROWS), ROWS)
                    x = [jnp.concatenate([upd[part, t, rows, :] for t in range(TILES)], 1) for part in range(2)]
                    first = (b * 4 + e) * 2 * ROWS
                    ref[first : first + 2 * ROWS, :] = (jnp.concatenate(x, 0) * scale).astype(BF16)
                planes = []
                for k in range(3):
                    rows = [pl.ds(pl.multiple_of(chunk * 4 * ROWS + g * ROWS, ROWS), ROWS) for g in range(4)]
                    planes.append(jnp.concatenate([num[k, x, :] for x in rows], 1))
                first = 4 * 2 * ROWS * BLOCKS + e * 4 * ROWS
                ref[first : first + 4 * ROWS, :] = jnp.concatenate(planes + [jnp.zeros_like(planes[0])], 0).astype(BF16)


def visit_all(place, corners, bands, probe, amplitude):
    count = amplitude.shape[0]
    fore, back = dft_blocks(FRAME)
    amp_spec = pl.BlockSpec((PER_STEP, FRAME, FRAME), lambda i: (i, 0, 0))
    return pl.pallas_call(
        visit_kernel,
        grid=(count // PER_STEP,),
        in_specs=[SMEM, SMEM] + [VMEM] * 13 + [amp_spec],
        out_specs=[VMEM] * 2,
        out_shape=[jax.ShapeDtypeStruct((SUMS, COLUMNS), BF16)] * 2,
        scratch_shapes=[
            pltpu.VMEM((2, TILES, BAND, LANES), F32),
            pltpu.VMEM((2, TILES, BAND, LANES), F32),
            pltpu.VMEM((3, FRAME, FRAME), F32),
        ],
        compiler_params=pltpu.CompilerParams(vmem_limit_bytes=48 << 20),
        cost_estimate=pl.CostEstimate(flops=count * 16 * 2 * FRAME**3, bytes_accessed=16 << 20, transcendentals=0),
    )(place, corners, *bands, probe, fore, back, amplitude)


def slab_along(value, steps):
    count = lax.axis_size("slab")
    first, last = (max(0, -steps), min(count, count - steps))
    return lax.ppermute(value, "slab", [(source, source + steps) for source in range(first, last)])


def slab_swap(value, bit):
    return lax.ppermute(value, "slab", [(i, i ^ bit) for i in range(lax.axis_size("slab"))])


def z_along(value, steps):
    return lax.ppermute(value, "view", [(i, (i + 2 * steps) % VIEWS) for i in range(VIEWS)])


def core_swap(value):
    return lax.ppermute(value, "view", [(i, i ^ 1) for i in range(VIEWS)])


def z_sum(value):
    return value[0] + z_along(value[1], 1) + z_along(value[2], 2) + z_along(value[3], 3)


def z_gather(value):
    return jnp.concatenate([value] + [z_along(value, d) for d in (1, 2, 3)], 0)


def on_device(object_field, probe, amplitude, offsets):
    layers = object_field.shape[1]
    view = lax.axis_index("view")
    place = jnp.stack([view // 2, view % 2, view * layers]).astype(jnp.int32)
    corners = offsets - jnp.stack([lax.axis_index("slab") * SLAB, 0]).astype(jnp.int32)

    received = core_swap(project(place, object_field, 1))
    piece = z_sum(project(place, object_field, 0) + received).astype(BF16)
    mine = z_gather(piece)
    bands = [mine] + [slab_along(mine, -k) for k in range(1, BLOCKS)]
    bands = bands + [core_swap(x) for x in bands]

    mine, theirs = visit_all(place, corners, bands, probe, amplitude)
    both = mine.astype(F32) + core_swap(theirs).astype(F32)
    terms = [both[k * SLAB : (k + 1) * SLAB] for k in range(BLOCKS)]
    update = terms[0]
    for k in range(1, BLOCKS):
        update = update + slab_along(terms[k].astype(BF16), k).astype(F32)
    update = z_gather(z_sum(update.reshape(4, 2 * ROWS, COLUMNS)).astype(BF16))
    object_new = spread(place, update, core_swap(update), object_field)

    totals = z_sum(both[BLOCKS * SLAB :].reshape(4, 4 * ROWS, COLUMNS)[:, : 3 * ROWS])
    for bit in (1, 2, 4, 8):
        totals = totals + slab_swap(totals, bit)
    ratio = (totals[: 2 * ROWS].reshape(2, ROWS, COLUMNS) / totals[2 * ROWS :]).reshape(2 * ROWS, COLUMNS)
    ratio = z_gather(ratio.astype(BF16))
    probe_step = join(place, ratio, core_swap(ratio))
    return object_new, probe_step


def solution(mesh):
    return jax.shard_map(
        on_device,
        mesh=mesh,
        in_specs=(P(None, "view", "slab", None), P(), P(("slab", "view"), None, None), P(("slab", "view"), None)),
        out_specs=(P(None, "view", "slab", None), P()),
        check_vma=False,
    )
```

```python
import functools
import math

import jax
import jax.numpy as jnp
import ml_dtypes
import numpy as np
from jax import lax
from jax.experimental import pallas as pl
from jax.experimental.pallas import tpu as pltpu
from jax.sharding import PartitionSpec as P

F32 = jnp.float32
BF16 = jnp.bfloat16
FRAME = 256
LANES = 128
SLAB = 64
VIEWS = 8
ROWS = SLAB // VIEWS
COLUMNS = 1024
TILES = COLUMNS // LANES
BLOCKS = 5
BAND = BLOCKS * SLAB
PER_STEP = 8
SUMS = BLOCKS * SLAB + 4 * 3 * ROWS
VMEM = pl.BlockSpec(memory_space=pltpu.VMEM)
SMEM = pl.BlockSpec(memory_space=pltpu.SMEM)


def dft_blocks(order):
    index = np.arange(order, dtype=np.int32)
    product = index[:, None] * index[None, :] % order
    angle = product.astype(np.float32) * np.float32(-2.0 * math.pi / order)
    factor = np.float32(1.0 / math.sqrt(order))
    c, s = np.cos(angle) * factor, np.sin(angle) * factor
    fore = np.block([[c, -s], [s, c]]).astype(ml_dtypes.bfloat16)
    back = np.block([[c, s], [-s, c]]).astype(ml_dtypes.bfloat16)
    return fore, back


def tiles_of(value):
    return [value[:, t * LANES : (t + 1) * LANES] for t in range(TILES)]


def to_right(tiles, steps):
    lane = lax.broadcasted_iota(jnp.int32, tiles[0].shape, 1)
    turned = [pltpu.roll(x, steps, 1) for x in tiles]
    return [jnp.where(lane >= steps, x, before) for x, before in zip(turned, [jnp.zeros_like(tiles[0])] + turned)]


def to_left(tiles, steps):
    lane = lax.broadcasted_iota(jnp.int32, tiles[0].shape, 1)
    turned = [pltpu.roll(x, (LANES - steps) % LANES, 1) for x in tiles]
    return [jnp.where(lane < LANES - steps, x, after) for x, after in zip(turned, turned[1:] + [jnp.zeros_like(tiles[0])])]


def chunk_at(place, half, e):
    return 4 * ((place[1] + half) % 2) + (place[0] + e) % 4


def rows_at(place, half, i):
    return pl.ds(pl.multiple_of((4 * ((place[1] + half) % 2) + i) * ROWS, ROWS), ROWS)


def project_kernel(half, place, field_ref, out_ref, held, sems):
    layers = field_ref.shape[1]
    copies = []
    for e in range(4):
        rows = pl.ds(pl.multiple_of(chunk_at(place, half, e) * ROWS, ROWS), ROWS)
        copies.append(pltpu.make_async_copy(field_ref.at[:, :, rows, :], held.at[e], sems.at[e]))
        copies[-1].start()
    for e in range(4):
        copies[e].wait()
        values = [tiles_of(jnp.concatenate([held[e, 0, k], held[e, 1, k]], 0)) for k in range(layers)]
        steps = 1
        while len(values) > 1:
            moved = [to_right(x, steps) for x in values[1::2]]
            values = [[a + b for a, b in zip(x, y)] for x, y in zip(values[0::2], moved)]
            steps *= 2
        for t, x in enumerate(to_right(values[0], place[2])):
            out_ref[e, :, t * LANES : (t + 1) * LANES] = x


def project(place, field, half):
    layers = field.shape[1]
    return pl.pallas_call(
        functools.partial(project_kernel, half),
        in_specs=[SMEM, pl.BlockSpec(memory_space=pl.ANY)],
        out_specs=VMEM,
        out_shape=jax.ShapeDtypeStruct((4, 2 * ROWS, COLUMNS), F32),
        scratch_shapes=[pltpu.VMEM((4, 2, layers, ROWS, COLUMNS), F32), pltpu.SemaphoreType.DMA((4,))],
        compiler_params=pltpu.CompilerParams(vmem_limit_bytes=60 << 20),
        cost_estimate=pl.CostEstimate(flops=layers * 4 * 16 * 1024 * 6, bytes_accessed=12 << 20, transcendentals=0),
    )(place, field)


def spread_kernel(place, mine_ref, theirs_ref, field_ref, out_ref, held, sems):
    layers = field_ref.shape[1]
    copies = []
    for half, ref in enumerate((mine_ref, theirs_ref)):
        for i in range(4):
            rows, slot = rows_at(place, half, i), half * 4 + i
            base = to_left(tiles_of(ref[i * 2 * ROWS : (i + 1) * 2 * ROWS, :].astype(F32)), place[2])
            for k in range(layers):
                for t, x in enumerate(to_left(base, k) if k else base):
                    columns = slice(t * LANES, (t + 1) * LANES)
                    for part in range(2):
                        held[slot, part, k, :, columns] = field_ref[part, k, rows, columns] + x[part * ROWS : (part + 1) * ROWS]
            copies.append(pltpu.make_async_copy(held.at[slot], out_ref.at[:, :, rows, :], sems.at[slot]))
            copies[-1].start()
    for copy in copies:
        copy.wait()


def spread(place, mine, theirs, field):
    layers = field.shape[1]
    return pl.pallas_call(
        spread_kernel,
        in_specs=[SMEM, VMEM, VMEM, VMEM],
        out_specs=pl.BlockSpec(memory_space=pl.ANY),
        out_shape=jax.ShapeDtypeStruct(field.shape, F32),
        scratch_shapes=[pltpu.VMEM((VIEWS, 2, layers, ROWS, COLUMNS), F32), pltpu.SemaphoreType.DMA((VIEWS,))],
        compiler_params=pltpu.CompilerParams(vmem_limit_bytes=40 << 20),
        cost_estimate=pl.CostEstimate(flops=layers * 8 * 16 * 1024 * 4, bytes_accessed=16 << 20, transcendentals=0),
    )(place, mine, theirs, field)


def join_kernel(place, mine_ref, theirs_ref, out_ref):
    for half, ref in enumerate((mine_ref, theirs_ref)):
        for j in range(4):
            first = chunk_at(place, half, 4 - j) * (FRAME // VIEWS)
            for part in range(2):
                x = ref[j * 2 * ROWS : (j + 1) * 2 * ROWS, :][part * ROWS : (part + 1) * ROWS]
                for g in range(4):
                    rows = pl.ds(pl.multiple_of(first + g * ROWS, ROWS), ROWS)
                    out_ref[part, rows, :] = x[:, g * FRAME : (g + 1) * FRAME].astype(F32)


def join(place, mine, theirs):
    return pl.pallas_call(
        join_kernel,
        in_specs=[SMEM, VMEM, VMEM],
        out_specs=VMEM,
        out_shape=jax.ShapeDtypeStruct((2, FRAME, FRAME), F32),
        cost_estimate=pl.CostEstimate(flops=1000, bytes_accessed=1 << 20, transcendentals=0),
    )(place, mine, theirs)


def dot(left, right):
    return jnp.dot(left, right, preferred_element_type=F32)


def visit_kernel(place, off_ref, *refs):
    bands, (theirs_band, probe_ref, fore_ref, back_ref, amp_ref, mine_ref, theirs_ref, band, upd, num) = refs[:BLOCKS], refs[BLOCKS:]
    step = pl.program_id(0)

    @pl.when(step == 0)
    def _():
        for i in range(2 * BLOCKS):
            half, block = i // BLOCKS, i % BLOCKS
            for j in range(4):
                first = (block * 4 * half + j) * 2 * ROWS
                x = (theirs_band if half else bands[block])[first : first + 2 * ROWS, :].astype(F32)
                first = pl.multiple_of(block * SLAB + chunk_at(place, half, 4 - j) * ROWS, ROWS)
                for part in range(2):
                    for t in range(TILES):
                        band[part, t, pl.ds(first, ROWS), :] = x[part * ROWS : (part + 1) * ROWS, t * LANES : (t + 1) * LANES]
        upd[...] = jnp.zeros_like(upd)
        num[...] = jnp.zeros_like(num)

    lane = lax.broadcasted_iota(jnp.int32, (FRAME, LANES), 1)

    def corner(j):
        p = step * PER_STEP + j
        r, c = off_ref[p, 0], off_ref[p, 1]
        q, m = c // LANES, c % LANES
        return r, (q, q + 1, jnp.minimum(q + 2, TILES - 1)), m

    def patch_of(part, r, q, m):
        turn = (LANES - m) % LANES
        tiles = [pltpu.roll(band[part, t, pl.ds(r, FRAME), :], turn, 1) for t in q]
        keep = lane < LANES - m
        return jnp.concatenate([jnp.where(keep, tiles[0], tiles[1]), jnp.where(keep, tiles[1], tiles[2])], 1)

    def add_to(part, value, r, q, m):
        left = pltpu.roll(value[:, :LANES], m, 1)
        right = pltpu.roll(value[:, LANES:], m, 1)
        keep = lane >= m
        terms = [jnp.where(keep, left, 0.0), jnp.where(keep, right, left), jnp.where(keep, 0.0, right)]
        for t, x in zip(q, terms):
            upd[part, t, pl.ds(r, FRAME), :] += x

    pr, pi = probe_ref[0], probe_ref[1]
    corners = [corner(j) for j in range(PER_STEP)]
    kept = [dict() for _ in range(PER_STEP)]

    def enter(j, at):
        r, q, m = corners[j]
        at["a"], at["b"] = a, b = patch_of(0, r, q, m), patch_of(1, r, q, m)
        at["er"], at["ei"] = pr * a - pi * b, pr * b + pi * a

    def rows_out(j, at):
        h = dot(fore_ref[...], jnp.concatenate([at["er"], at["ei"]], 0).astype(BF16))
        at["half"] = jnp.concatenate([h[:FRAME], h[FRAME:]], 1).astype(BF16)

    def columns_out(j, at):
        at["far"] = dot(at["half"], back_ref[...])

    def fix(j, at):
        fr, fi = at["far"][:, :FRAME], at["far"][:, FRAME:]
        factor = amp_ref[j] * lax.rsqrt(fr * fr + fi * fi + 0.25)
        at["fixed"] = jnp.concatenate([fr * factor, fi * factor], 1).astype(BF16)

    def columns_back(j, at):
        h = dot(at["fixed"], fore_ref[...])
        at["back"] = jnp.concatenate([h[:, :FRAME], h[:, FRAME:]], 0).astype(BF16)

    def rows_back(j, at):
        at["new"] = dot(back_ref[...], at["back"])

    def leave(j, at):
        a, b = at["a"], at["b"]
        dr, di = at["new"][:FRAME] - at["er"], at["new"][FRAME:] - at["ei"]
        r, q, m = corners[j]
        add_to(0, pr * dr + pi * di, r, q, m)
        add_to(1, pr * di - pi * dr, r, q, m)
        num[0] += a * dr + b * di
        num[1] += a * di - b * dr
        num[2] += a * a + b * b

    stages = (enter, rows_out, columns_out, fix, columns_back, rows_back, leave)
    for tick in range(2 * (PER_STEP - 1) + len(stages)):
        due = [(tick - 2 * j, j) for j in range(PER_STEP) if 0 <= tick - 2 * j < len(stages)]
        for k, j in due:
            stages[k](j, kept[j])

    @pl.when(step == pl.num_programs(0) - 1)
    def _():
        peak = jnp.max(pr * pr + pi * pi) + 1e-06
        scale = 0.5 / jnp.full((2 * ROWS, COLUMNS), peak, F32)
        for half, ref in enumerate((mine_ref, theirs_ref)):
            for i in range(4):
                for b in range(BLOCKS):
                    rows = pl.ds(pl.multiple_of(b * SLAB + (4 * ((place[1] + half) % 2) + i) * ROWS, ROWS), ROWS)
                    x = [jnp.concatenate([upd[part, t, rows, :] for t in range(TILES)], 1) for part in range(2)]
                    first = (b * 4 + i) * 2 * ROWS
                    ref[first : first + 2 * ROWS, :] = (jnp.concatenate(x, 0) * scale).astype(BF16)
            planes = []
            for e in range(4):
                for k in range(3):
                    first = chunk_at(place, half, e) * 4 * ROWS
                    rows = [pl.ds(pl.multiple_of(first + g * ROWS, ROWS), ROWS) for g in range(4)]
                    planes.append(jnp.concatenate([num[k, x, :] for x in rows], 1))
            ref[BLOCKS * SLAB : SUMS, :] = jnp.concatenate(planes, 0).astype(BF16)


def visit_all(place, corners, bands, others, probe, amplitude):
    count = amplitude.shape[0]
    fore, back = dft_blocks(FRAME)
    amp_spec = pl.BlockSpec((PER_STEP, FRAME, FRAME), lambda i: (i, 0, 0))
    return pl.pallas_call(
        visit_kernel,
        grid=(count // PER_STEP,),
        in_specs=[SMEM, SMEM] + [VMEM] * 9 + [amp_spec],
        out_specs=[VMEM] * 2,
        out_shape=[jax.ShapeDtypeStruct((SUMS, COLUMNS), BF16)] * 2,
        scratch_shapes=[
            pltpu.VMEM((2, TILES, BAND, LANES), F32),
            pltpu.VMEM((2, TILES, BAND, LANES), F32),
            pltpu.VMEM((3, FRAME, FRAME), F32),
        ],
        compiler_params=pltpu.CompilerParams(vmem_limit_bytes=48 << 20),
        cost_estimate=pl.CostEstimate(flops=count * 16 * 2 * FRAME**3, bytes_accessed=16 << 20, transcendentals=0),
    )(place, corners, *bands, others, probe, fore, back, amplitude)


def slab_along(value, steps):
    count = lax.axis_size("slab")
    first, last = (max(0, -steps), min(count, count - steps))
    return lax.ppermute(value, "slab", [(source, source + steps) for source in range(first, last)])


def slab_ring(value, axis, steps):
    moves = []
    for i in range(lax.axis_size("slab")):
        y, x = divmod(i, 4)
        moves.append((i, 4 * y + (x + steps) % 4 if axis == 0 else 4 * ((y + steps) % 4) + x))
    return lax.ppermute(value, "slab", moves)


def ring_sum(value, axis):
    one, two, three = (slab_ring(value, axis, k) for k in (1, 2, 3))
    return (value + two) + (one + three)


def z_along(value, steps):
    return lax.ppermute(value, "view", [(i, (i + 2 * steps) % VIEWS) for i in range(VIEWS)])


def core_swap(value):
    return lax.ppermute(value, "view", [(i, i ^ 1) for i in range(VIEWS)])


def z_sum(value):
    return value[0] + z_along(value[1], 1) + z_along(value[2], 2) + z_along(value[3], 3)


def z_gather(value):
    return jnp.concatenate([value] + [z_along(value, d) for d in (1, 2, 3)], 0)


def on_device(object_field, probe, amplitude, offsets):
    layers = object_field.shape[1]
    view = lax.axis_index("view")
    place = jnp.stack([view // 2, view % 2, view * layers]).astype(jnp.int32)
    corners = offsets - jnp.stack([lax.axis_index("slab") * SLAB, 0]).astype(jnp.int32)

    received = core_swap(project(place, object_field, 1))
    piece = z_sum(project(place, object_field, 0) + received).astype(BF16)
    mine = z_gather(piece)
    bands = [mine] + [slab_along(mine, -k) for k in range(1, BLOCKS)]
    others = core_swap(jnp.concatenate(bands, 0))

    mine, theirs = visit_all(place, corners, bands, others, probe, amplitude)
    both = mine.astype(F32) + core_swap(theirs).astype(F32)
    update = both[:SLAB]
    for k in range(1, BLOCKS):
        update = update + slab_along(both[k * SLAB : (k + 1) * SLAB].astype(BF16), k).astype(F32)
    totals = z_sum(both[BLOCKS * SLAB :].reshape(4, 3 * ROWS, COLUMNS))
    update, totals = lax.optimization_barrier((update, totals))
    sent = update.astype(BF16)
    update = update + sum(z_along(sent, d).astype(F32) for d in (1, 2, 3))
    totals = ring_sum(totals, 0)
    update, totals = lax.optimization_barrier((update, totals))
    update_there = core_swap(update)
    totals = ring_sum(totals, 1)
    ratio = (totals[: 2 * ROWS].reshape(2, ROWS, COLUMNS) / totals[2 * ROWS :]).reshape(2 * ROWS, COLUMNS)
    update_there, ratio = lax.optimization_barrier((update_there, ratio))
    ratio = z_gather(ratio.astype(BF16))
    object_new = spread(place, update, update_there, object_field)
    object_new, ratio = lax.optimization_barrier((object_new, ratio))
    probe_step = join(place, ratio, core_swap(ratio))
    return object_new, probe_step


def solution(mesh):
    return jax.shard_map(
        on_device,
        mesh=mesh,
        in_specs=(P(None, "view", "slab", None), P(), P(("slab", "view"), None, None), P(("slab", "view"), None)),
        out_specs=(P(None, "view", "slab", None), P()),
        check_vma=False,
    )
```

```python
import functools
import math

import jax
import jax.numpy as jnp
import ml_dtypes
import numpy as np
from jax import lax
from jax.experimental import pallas as pl
from jax.experimental.pallas import tpu as pltpu
from jax.sharding import PartitionSpec as P

F32 = jnp.float32
BF16 = jnp.bfloat16
FRAME = 256
LANES = 128
SLAB = 64
VIEWS = 8
ROWS = SLAB // VIEWS
COLUMNS = 1024
TILES = COLUMNS // LANES
BLOCKS = 5
BAND = BLOCKS * SLAB
PER_STEP = 8
VMEM = pl.BlockSpec(memory_space=pltpu.VMEM)
SMEM = pl.BlockSpec(memory_space=pltpu.SMEM)


def dft_blocks(order):
    index = np.arange(order, dtype=np.int32)
    product = index[:, None] * index[None, :] % order
    angle = product.astype(np.float32) * np.float32(-2.0 * math.pi / order)
    factor = np.float32(1.0 / math.sqrt(order))
    c, s = np.cos(angle) * factor, np.sin(angle) * factor
    fore = np.block([[c, -s], [s, c]]).astype(ml_dtypes.bfloat16)
    back = np.block([[c, s], [-s, c]]).astype(ml_dtypes.bfloat16)
    return fore, back


def tiles_of(value):
    return [value[:, t * LANES : (t + 1) * LANES] for t in range(TILES)]


def to_right(tiles, steps):
    lane = lax.broadcasted_iota(jnp.int32, tiles[0].shape, 1)
    turned = [pltpu.roll(x, steps, 1) for x in tiles]
    return [jnp.where(lane >= steps, x, before) for x, before in zip(turned, [jnp.zeros_like(tiles[0])] + turned)]


def to_left(tiles, steps):
    lane = lax.broadcasted_iota(jnp.int32, tiles[0].shape, 1)
    turned = [pltpu.roll(x, (LANES - steps) % LANES, 1) for x in tiles]
    return [jnp.where(lane < LANES - steps, x, after) for x, after in zip(turned, turned[1:] + [jnp.zeros_like(tiles[0])])]


def chunk_at(place, half, e):
    return 4 * ((place[1] + half) % 2) + (place[0] + e) % 4


def rows_of(place, e, c):
    return pl.ds(pl.multiple_of(((place[0] + e) % 4 * 2 + c) * ROWS, ROWS), ROWS)


def project_kernel(half, place, field_ref, out_ref, held, sems):
    layers = field_ref.shape[1]
    copies = []
    for e in range(4):
        rows = pl.ds(pl.multiple_of(chunk_at(place, half, e) * ROWS, ROWS), ROWS)
        copies.append(pltpu.make_async_copy(field_ref.at[:, :, rows, :], held.at[e], sems.at[e]))
        copies[-1].start()
    for e in range(4):
        copies[e].wait()
        values = [tiles_of(jnp.concatenate([held[e, 0, k], held[e, 1, k]], 0)) for k in range(layers)]
        steps = 1
        while len(values) > 1:
            moved = [to_right(x, steps) for x in values[1::2]]
            values = [[a + b for a, b in zip(x, y)] for x, y in zip(values[0::2], moved)]
            steps *= 2
        for t, x in enumerate(to_right(values[0], place[2])):
            out_ref[e, :, t * LANES : (t + 1) * LANES] = x


def project(place, field, half):
    layers = field.shape[1]
    return pl.pallas_call(
        functools.partial(project_kernel, half),
        in_specs=[SMEM, pl.BlockSpec(memory_space=pl.ANY)],
        out_specs=VMEM,
        out_shape=jax.ShapeDtypeStruct((4, 2 * ROWS, COLUMNS), F32),
        scratch_shapes=[pltpu.VMEM((4, 2, layers, ROWS, COLUMNS), F32), pltpu.SemaphoreType.DMA((4,))],
        compiler_params=pltpu.CompilerParams(vmem_limit_bytes=60 << 20),
        cost_estimate=pl.CostEstimate(flops=layers * 4 * 16 * 1024 * 6, bytes_accessed=12 << 20, transcendentals=0),
    )(place, field)


def spread_kernel(place, mine_ref, theirs_ref, field_ref, out_ref, held, sems):
    layers = field_ref.shape[1]
    copies = []
    for slot in range(VIEWS):
        j, c = divmod(slot, 2)
        rows, first = rows_of(place, 4 - j, c), slot * 2 * ROWS
        update = jnp.where(place[1] == 0, mine_ref[first : first + 2 * ROWS, :].astype(F32), theirs_ref[first : first + 2 * ROWS, :].astype(F32))
        base = to_left(tiles_of(update), place[2])
        for k in range(layers):
            for t, x in enumerate(to_left(base, k) if k else base):
                columns = slice(t * LANES, (t + 1) * LANES)
                for part in range(2):
                    held[slot, part, k, :, columns] = field_ref[part, k, rows, columns] + x[part * ROWS : (part + 1) * ROWS]
        copies.append(pltpu.make_async_copy(held.at[slot], out_ref.at[:, :, rows, :], sems.at[slot]))
        copies[-1].start()
    for copy in copies:
        copy.wait()


def spread(place, mine, theirs, field):
    layers = field.shape[1]
    return pl.pallas_call(
        spread_kernel,
        in_specs=[SMEM, VMEM, VMEM, VMEM],
        out_specs=pl.BlockSpec(memory_space=pl.ANY),
        out_shape=jax.ShapeDtypeStruct(field.shape, F32),
        scratch_shapes=[pltpu.VMEM((VIEWS, 2, layers, ROWS, COLUMNS), F32), pltpu.SemaphoreType.DMA((VIEWS,))],
        compiler_params=pltpu.CompilerParams(vmem_limit_bytes=40 << 20),
        cost_estimate=pl.CostEstimate(flops=layers * 8 * 16 * 1024 * 4, bytes_accessed=16 << 20, transcendentals=0),
    )(place, mine, theirs, field)


def join_kernel(place, mine_ref, theirs_ref, out_ref):
    for j in range(4):
        for part in range(2):
            first = (j * 2 + part) * 2 * ROWS
            own, other = mine_ref[first : first + 2 * ROWS, :].astype(F32), theirs_ref[first : first + 2 * ROWS, :].astype(F32)
            x = jnp.where(place[1] == 1, own, other)
            for c in range(2):
                for g in range(4):
                    start = (place[3] + 4 - j) % 4 * SLAB + c * 4 * ROWS + g * ROWS
                    piece = x[c * ROWS : (c + 1) * ROWS, g * FRAME : (g + 1) * FRAME]
                    out_ref[part, pl.ds(pl.multiple_of(start, ROWS), ROWS), :] = piece


def join(place, mine, theirs):
    return pl.pallas_call(
        join_kernel,
        in_specs=[SMEM, VMEM, VMEM],
        out_specs=VMEM,
        out_shape=jax.ShapeDtypeStruct((2, FRAME, FRAME), F32),
        cost_estimate=pl.CostEstimate(flops=1000, bytes_accessed=1 << 20, transcendentals=0),
    )(place, mine, theirs)


def dot(left, right):
    return jnp.dot(left, right, preferred_element_type=F32)


def visit_kernel(place, off_ref, *refs):
    bands, (probe_ref, fore_ref, back_ref, amp_ref, update_ref, sums_ref, band, upd, num) = refs[: 2 * BLOCKS], refs[2 * BLOCKS :]
    step = pl.program_id(0)

    @pl.when(step == 0)
    def _():
        for i, ref in enumerate(bands):
            half, block = divmod(i, BLOCKS)
            for j in range(4):
                x = ref[j * 2 * ROWS : (j + 1) * 2 * ROWS, :].astype(F32)
                x = jnp.where(place[4] + block < place[5], x, 0.0)
                first = pl.multiple_of(block * SLAB + chunk_at(place, half, 4 - j) * ROWS, ROWS)
                for part in range(2):
                    for t in range(TILES):
                        band[part, t, pl.ds(first, ROWS), :] = x[part * ROWS : (part + 1) * ROWS, t * LANES : (t + 1) * LANES]
        upd[...] = jnp.zeros_like(upd)
        num[...] = jnp.zeros_like(num)

    lane = lax.broadcasted_iota(jnp.int32, (FRAME, LANES), 1)

    def corner(j):
        p = step * PER_STEP + j
        r, c = off_ref[p, 0], off_ref[p, 1]
        q, m = c // LANES, c % LANES
        return r, (q, q + 1, jnp.minimum(q + 2, TILES - 1)), m

    def patch_of(part, r, q, m):
        turn = (LANES - m) % LANES
        tiles = [pltpu.roll(band[part, t, pl.ds(r, FRAME), :], turn, 1) for t in q]
        keep = lane < LANES - m
        return jnp.concatenate([jnp.where(keep, tiles[0], tiles[1]), jnp.where(keep, tiles[1], tiles[2])], 1)

    def add_to(part, value, r, q, m):
        left = pltpu.roll(value[:, :LANES], m, 1)
        right = pltpu.roll(value[:, LANES:], m, 1)
        keep = lane >= m
        terms = [jnp.where(keep, left, 0.0), jnp.where(keep, right, left), jnp.where(keep, 0.0, right)]
        for t, x in zip(q, terms):
            upd[part, t, pl.ds(r, FRAME), :] += x

    pr, pi = probe_ref[0], probe_ref[1]
    corners = [corner(j) for j in range(PER_STEP)]
    kept = [dict() for _ in range(PER_STEP)]

    def enter(j, at):
        r, q, m = corners[j]
        at["a"], at["b"] = a, b = patch_of(0, r, q, m), patch_of(1, r, q, m)
        at["er"], at["ei"] = pr * a - pi * b, pr * b + pi * a

    def rows_out(j, at):
        h = dot(fore_ref[...], jnp.concatenate([at["er"], at["ei"]], 0).astype(BF16))
        at["half"] = jnp.concatenate([h[:FRAME], h[FRAME:]], 1).astype(BF16)

    def columns_out(j, at):
        at["far"] = dot(at["half"], back_ref[...])

    def fix(j, at):
        fr, fi = at["far"][:, :FRAME], at["far"][:, FRAME:]
        factor = amp_ref[j] * lax.rsqrt(fr * fr + fi * fi + 0.25)
        at["fixed"] = jnp.concatenate([fr * factor, fi * factor], 1).astype(BF16)

    def columns_back(j, at):
        h = dot(at["fixed"], fore_ref[...])
        at["back"] = jnp.concatenate([h[:, :FRAME], h[:, FRAME:]], 0).astype(BF16)

    def rows_back(j, at):
        at["new"] = dot(back_ref[...], at["back"])

    def leave(j, at):
        a, b = at["a"], at["b"]
        dr, di = at["new"][:FRAME] - at["er"], at["new"][FRAME:] - at["ei"]
        r, q, m = corners[j]
        add_to(0, pr * dr + pi * di, r, q, m)
        add_to(1, pr * di - pi * dr, r, q, m)
        num[0] += a * dr + b * di
        num[1] += a * di - b * dr
        num[2] += a * a + b * b

    stages = (enter, rows_out, columns_out, fix, columns_back, rows_back, leave)
    for tick in range(2 * (PER_STEP - 1) + len(stages)):
        due = [(tick - 2 * j, j) for j in range(PER_STEP) if 0 <= tick - 2 * j < len(stages)]
        for k, j in due:
            stages[k](j, kept[j])

    @pl.when(step == pl.num_programs(0) - 1)
    def _():
        peak = jnp.max(pr * pr + pi * pi) + 1e-06
        scale = 0.5 / jnp.full((2 * ROWS, COLUMNS), peak, F32)
        for e in range(4):
            for b in range(BLOCKS):
                for c in range(2):
                    rows = pl.ds(pl.multiple_of(b * SLAB + ((place[0] + e) % 4 * 2 + c) * ROWS, ROWS), ROWS)
                    x = [jnp.concatenate([upd[part, t, rows, :] for t in range(TILES)], 1) for part in range(2)]
                    first = ((e * BLOCKS + b) * 2 + c) * 2 * ROWS
                    update_ref[first : first + 2 * ROWS, :] = (jnp.concatenate(x, 0) * scale).astype(BF16)
            planes = []
            for k in range(3):
                for c in range(2):
                    first = (place[3] + e) % 4 * SLAB + c * 4 * ROWS
                    rows = [pl.ds(pl.multiple_of(first + g * ROWS, ROWS), ROWS) for g in range(4)]
                    planes.append(jnp.concatenate([num[k, x, :] for x in rows], 1))
            sums_ref[e * 6 * ROWS : (e + 1) * 6 * ROWS, :] = jnp.concatenate(planes, 0).astype(BF16)


def visit_all(place, corners, bands, probe, amplitude):
    count = amplitude.shape[0]
    fore, back = dft_blocks(FRAME)
    amp_spec = pl.BlockSpec((PER_STEP, FRAME, FRAME), lambda i: (i, 0, 0))
    return pl.pallas_call(
        visit_kernel,
        grid=(count // PER_STEP,),
        in_specs=[SMEM, SMEM] + [VMEM] * 13 + [amp_spec],
        out_specs=[VMEM] * 2,
        out_shape=[
            jax.ShapeDtypeStruct((2 * BAND, COLUMNS), BF16),
            jax.ShapeDtypeStruct((4 * 6 * ROWS, COLUMNS), BF16),
        ],
        scratch_shapes=[
            pltpu.VMEM((2, TILES, BAND, LANES), F32),
            pltpu.VMEM((2, TILES, BAND, LANES), F32),
            pltpu.VMEM((3, FRAME, FRAME), F32),
        ],
        compiler_params=pltpu.CompilerParams(vmem_limit_bytes=48 << 20),
        cost_estimate=pl.CostEstimate(flops=count * 16 * 2 * FRAME**3, bytes_accessed=16 << 20, transcendentals=0),
    )(place, corners, *bands, probe, fore, back, amplitude)


def moved(value, cores, target):
    count = lax.axis_size("slab")
    moves = []
    for slab in range(count):
        for z in range(4):
            for core in cores:
                to_slab, to_z, to_core = target(slab, z, core)
                moves.append((slab * VIEWS + z * 2 + core, to_slab % count * VIEWS + to_z % 4 * 2 + to_core))
    return lax.ppermute(value, ("slab", "view"), moves)


def core_swap(value, cores=(0, 1)):
    return moved(value, cores, lambda slab, z, core: (slab, z, 1 - core))


def slab_along(value, steps, cores=(0, 1)):
    return moved(value, cores, lambda slab, z, core: (slab + steps, z, core))


def z_along(value, steps, cores=(0, 1)):
    return moved(value, cores, lambda slab, z, core: (slab, z + steps, core))


def x_along(value, steps, cores=(0, 1)):
    return moved(value, cores, lambda slab, z, core: (slab // 4 * 4 + (slab + steps) % 4, z, core))


def y_along(value, steps, cores=(0, 1)):
    return moved(value, cores, lambda slab, z, core: (slab + 4 * steps, z, core))


def ring_parts(along, parts, cores):
    return parts[0] + sum(along(parts[e].astype(BF16), e, cores).astype(F32) for e in (1, 2, 3))


def ring_total(along, value, cores):
    one, two, three = (along(value, e, cores) for e in (1, 2, 3))
    return (value + two) + (one + three)


def ring_gather(along, value, cores):
    return jnp.concatenate([value] + [along(value, e, cores) for e in (1, 2, 3)], 0)


def on_device(object_field, probe, amplitude, offsets):
    layers = object_field.shape[1]
    view, slab = lax.axis_index("view"), lax.axis_index("slab")
    count = lax.axis_size("slab")
    place = jnp.stack([view >> 1, view & 1, view * layers, slab & 3, slab, count]).astype(jnp.int32)
    corners = offsets - jnp.stack([slab * SLAB, 0]).astype(jnp.int32)

    received = core_swap(project(place, object_field, 1))
    shares = project(place, object_field, 0) + received
    piece = shares[0] + sum(z_along(shares[e], e) for e in (1, 2, 3))
    mine = ring_gather(z_along, piece.astype(BF16), (0, 1))
    bands = [mine] + [slab_along(mine, -k) for k in range(1, BLOCKS)]
    bands = bands + [core_swap(x) for x in bands]
    update, sums = visit_all(place, corners, bands, probe, amplitude)

    update = update.astype(F32) + core_swap(update, (1,)).astype(F32)
    sums = sums.astype(F32) + core_swap(sums, (0,)).astype(F32)
    update = ring_parts(z_along, update.reshape(4, 2 * BAND // 4, COLUMNS), (0,))
    sums = ring_parts(x_along, sums.reshape(4, 6 * ROWS, COLUMNS), (1,))
    blocks = update.reshape(BLOCKS, 4 * ROWS, COLUMNS)
    update = blocks[0]
    for k in range(1, BLOCKS):
        term = slab_along(blocks[k].astype(BF16), k, (0,)).astype(F32)
        update = update + jnp.where(slab >= k, term, 0.0)
    sums = ring_total(z_along, sums, (1,))
    update = ring_gather(z_along, update.astype(BF16), (0,))
    sums = ring_total(y_along, sums, (1,))
    planes = sums.reshape(3, 2 * ROWS, COLUMNS)
    ratio = (planes[:2] / planes[2]).reshape(4 * ROWS, COLUMNS).astype(BF16)
    update_there = core_swap(update, (0,))
    ratio = ring_gather(x_along, ratio, (1,))
    object_new = spread(place, update, update_there, object_field)
    object_new, ratio = lax.optimization_barrier((object_new, ratio))
    probe_step = join(place, ratio, core_swap(ratio, (1,)))
    return object_new, probe_step


def solution(mesh):
    return jax.shard_map(
        on_device,
        mesh=mesh,
        in_specs=(P(None, "view", "slab", None), P(), P(("slab", "view"), None, None), P(("slab", "view"), None)),
        out_specs=(P(None, "view", "slab", None), P()),
        check_vma=False,
    )
```

```python
import functools
import math

import jax
import jax.numpy as jnp
import ml_dtypes
import numpy as np
from jax import lax
from jax.experimental import pallas as pl
from jax.experimental.pallas import tpu as pltpu
from jax.sharding import PartitionSpec as P

F32 = jnp.float32
BF16 = jnp.bfloat16
FRAME = 256
LANES = 128
SLAB = 64
VIEWS = 8
ROWS = SLAB // VIEWS
COLUMNS = 1024
TILES = COLUMNS // LANES
BLOCKS = 5
BAND = BLOCKS * SLAB
PER_STEP = 8
SUMS = BLOCKS * SLAB + 4 * 3 * ROWS
VMEM = pl.BlockSpec(memory_space=pltpu.VMEM)
SMEM = pl.BlockSpec(memory_space=pltpu.SMEM)


def dft_blocks(order):
    index = np.arange(order, dtype=np.int32)
    product = index[:, None] * index[None, :] % order
    angle = product.astype(np.float32) * np.float32(-2.0 * math.pi / order)
    factor = np.float32(1.0 / math.sqrt(order))
    c, s = np.cos(angle) * factor, np.sin(angle) * factor
    fore = np.block([[c, -s], [s, c]]).astype(ml_dtypes.bfloat16)
    back = np.block([[c, s], [-s, c]]).astype(ml_dtypes.bfloat16)
    return fore, back


def tiles_of(value):
    return [value[:, t * LANES : (t + 1) * LANES] for t in range(TILES)]


def to_right(tiles, steps):
    lane = lax.broadcasted_iota(jnp.int32, tiles[0].shape, 1)
    turned = [pltpu.roll(x, steps, 1) for x in tiles]
    return [jnp.where(lane >= steps, x, before) for x, before in zip(turned, [jnp.zeros_like(tiles[0])] + turned)]


def to_left(tiles, steps):
    lane = lax.broadcasted_iota(jnp.int32, tiles[0].shape, 1)
    turned = [pltpu.roll(x, (LANES - steps) % LANES, 1) for x in tiles]
    return [jnp.where(lane < LANES - steps, x, after) for x, after in zip(turned, turned[1:] + [jnp.zeros_like(tiles[0])])]


def chunk_at(place, half, e):
    return 4 * ((place[1] + half) % 2) + (place[0] + e) % 4


def rows_at(place, half, i):
    return pl.ds(pl.multiple_of((4 * ((place[1] + half) % 2) + i) * ROWS, ROWS), ROWS)


def project_kernel(half, place, field_ref, out_ref, held, sems):
    layers = field_ref.shape[1]
    copies = []
    for e in range(4):
        rows = pl.ds(pl.multiple_of(chunk_at(place, half, e) * ROWS, ROWS), ROWS)
        copies.append(pltpu.make_async_copy(field_ref.at[:, :, rows, :], held.at[e], sems.at[e]))
        copies[-1].start()
    for e in range(4):
        copies[e].wait()
        values = [tiles_of(jnp.concatenate([held[e, 0, k], held[e, 1, k]], 0)) for k in range(layers)]
        steps = 1
        while len(values) > 1:
            moved = [to_right(x, steps) for x in values[1::2]]
            values = [[a + b for a, b in zip(x, y)] for x, y in zip(values[0::2], moved)]
            steps *= 2
        for t, x in enumerate(to_right(values[0], place[2])):
            out_ref[e, :, t * LANES : (t + 1) * LANES] = x


def project(place, field, half):
    layers = field.shape[1]
    return pl.pallas_call(
        functools.partial(project_kernel, half),
        in_specs=[SMEM, pl.BlockSpec(memory_space=pl.ANY)],
        out_specs=VMEM,
        out_shape=jax.ShapeDtypeStruct((4, 2 * ROWS, COLUMNS), F32),
        scratch_shapes=[pltpu.VMEM((4, 2, layers, ROWS, COLUMNS), F32), pltpu.SemaphoreType.DMA((4,))],
        compiler_params=pltpu.CompilerParams(vmem_limit_bytes=60 << 20),
        cost_estimate=pl.CostEstimate(flops=layers * 4 * 16 * 1024 * 6, bytes_accessed=12 << 20, transcendentals=0),
    )(place, field)


def spread_kernel(place, mine_ref, theirs_ref, field_ref, out_ref, held, sems):
    layers = field_ref.shape[1]
    copies = []
    for half, ref in enumerate((mine_ref, theirs_ref)):
        for i in range(4):
            rows, slot = rows_at(place, half, i), half * 4 + i
            base = to_left(tiles_of(ref[i * 2 * ROWS : (i + 1) * 2 * ROWS, :].astype(F32)), place[2])
            for k in range(layers):
                for t, x in enumerate(to_left(base, k) if k else base):
                    columns = slice(t * LANES, (t + 1) * LANES)
                    for part in range(2):
                        held[slot, part, k, :, columns] = field_ref[part, k, rows, columns] + x[part * ROWS : (part + 1) * ROWS]
            copies.append(pltpu.make_async_copy(held.at[slot], out_ref.at[:, :, rows, :], sems.at[slot]))
            copies[-1].start()
    for copy in copies:
        copy.wait()


def spread(place, mine, theirs, field):
    layers = field.shape[1]
    return pl.pallas_call(
        spread_kernel,
        in_specs=[SMEM, VMEM, VMEM, VMEM],
        out_specs=pl.BlockSpec(memory_space=pl.ANY),
        out_shape=jax.ShapeDtypeStruct(field.shape, F32),
        scratch_shapes=[pltpu.VMEM((VIEWS, 2, layers, ROWS, COLUMNS), F32), pltpu.SemaphoreType.DMA((VIEWS,))],
        compiler_params=pltpu.CompilerParams(vmem_limit_bytes=40 << 20),
        cost_estimate=pl.CostEstimate(flops=layers * 8 * 16 * 1024 * 4, bytes_accessed=16 << 20, transcendentals=0),
    )(place, mine, theirs, field)


def join_kernel(place, mine_ref, theirs_ref, out_ref):
    for half, ref in enumerate((mine_ref, theirs_ref)):
        for part in range(2):
            for i in range(4):
                x = ref[(part * 4 + i) * ROWS : (part * 4 + i + 1) * ROWS, :]
                for g in range(4):
                    start = ((4 * ((place[1] + half) % 2) + i) * 4 + g) * ROWS
                    out_ref[part, pl.ds(pl.multiple_of(start, ROWS), ROWS), :] = x[:, g * FRAME : (g + 1) * FRAME]


def join(place, mine, theirs):
    return pl.pallas_call(
        join_kernel,
        in_specs=[SMEM, VMEM, VMEM],
        out_specs=VMEM,
        out_shape=jax.ShapeDtypeStruct((2, FRAME, FRAME), F32),
        cost_estimate=pl.CostEstimate(flops=1000, bytes_accessed=1 << 20, transcendentals=0),
    )(place, mine, theirs)


def dot(left, right):
    return jnp.dot(left, right, preferred_element_type=F32)


def visit_kernel(place, off_ref, *refs):
    bands, (probe_ref, fore_ref, back_ref, amp_ref, mine_ref, theirs_ref, band, upd, num) = refs[: 2 * BLOCKS], refs[2 * BLOCKS :]
    step = pl.program_id(0)

    @pl.when(step == 0)
    def _():
        for i, ref in enumerate(bands):
            half, block = divmod(i, BLOCKS)
            for j in range(4):
                x = ref[j * 2 * ROWS : (j + 1) * 2 * ROWS, :].astype(F32)
                x = jnp.where(place[3] + block < place[4], x, 0.0)
                first = pl.multiple_of(block * SLAB + chunk_at(place, half, 4 - j) * ROWS, ROWS)
                for part in range(2):
                    for t in range(TILES):
                        band[part, t, pl.ds(first, ROWS), :] = x[part * ROWS : (part + 1) * ROWS, t * LANES : (t + 1) * LANES]
        upd[...] = jnp.zeros_like(upd)
        num[...] = jnp.zeros_like(num)

    lane = lax.broadcasted_iota(jnp.int32, (FRAME, LANES), 1)

    def corner(j):
        p = step * PER_STEP + j
        r, c = off_ref[p, 0], off_ref[p, 1]
        q, m = c // LANES, c % LANES
        return r, (q, q + 1, jnp.minimum(q + 2, TILES - 1)), m

    def patch_of(part, r, q, m):
        turn = (LANES - m) % LANES
        tiles = [pltpu.roll(band[part, t, pl.ds(r, FRAME), :], turn, 1) for t in q]
        keep = lane < LANES - m
        return jnp.concatenate([jnp.where(keep, tiles[0], tiles[1]), jnp.where(keep, tiles[1], tiles[2])], 1)

    def add_to(part, value, r, q, m):
        left = pltpu.roll(value[:, :LANES], m, 1)
        right = pltpu.roll(value[:, LANES:], m, 1)
        keep = lane >= m
        terms = [jnp.where(keep, left, 0.0), jnp.where(keep, right, left), jnp.where(keep, 0.0, right)]
        for t, x in zip(q, terms):
            upd[part, t, pl.ds(r, FRAME), :] += x

    pr, pi = probe_ref[0], probe_ref[1]
    corners = [corner(j) for j in range(PER_STEP)]
    kept = [dict() for _ in range(PER_STEP)]

    def enter(j, at):
        r, q, m = corners[j]
        at["a"], at["b"] = a, b = patch_of(0, r, q, m), patch_of(1, r, q, m)
        at["er"], at["ei"] = pr * a - pi * b, pr * b + pi * a

    def rows_out(j, at):
        h = dot(fore_ref[...], jnp.concatenate([at["er"], at["ei"]], 0).astype(BF16))
        at["half"] = jnp.concatenate([h[:FRAME], h[FRAME:]], 1).astype(BF16)

    def columns_out(j, at):
        at["far"] = dot(at["half"], back_ref[...])

    def fix(j, at):
        fr, fi = at["far"][:, :FRAME], at["far"][:, FRAME:]
        factor = amp_ref[j] * lax.rsqrt(fr * fr + fi * fi + 0.25)
        at["fixed"] = jnp.concatenate([fr * factor, fi * factor], 1).astype(BF16)

    def columns_back(j, at):
        h = dot(at["fixed"], fore_ref[...])
        at["back"] = jnp.concatenate([h[:, :FRAME], h[:, FRAME:]], 0).astype(BF16)

    def rows_back(j, at):
        at["new"] = dot(back_ref[...], at["back"])

    def leave(j, at):
        a, b = at["a"], at["b"]
        dr, di = at["new"][:FRAME] - at["er"], at["new"][FRAME:] - at["ei"]
        r, q, m = corners[j]
        add_to(0, pr * dr + pi * di, r, q, m)
        add_to(1, pr * di - pi * dr, r, q, m)
        num[0] += a * dr + b * di
        num[1] += a * di - b * dr
        num[2] += a * a + b * b

    stages = (enter, rows_out, columns_out, fix, columns_back, rows_back, leave)
    for tick in range(2 * (PER_STEP - 1) + len(stages)):
        due = [(tick - 2 * j, j) for j in range(PER_STEP) if 0 <= tick - 2 * j < len(stages)]
        for k, j in due:
            stages[k](j, kept[j])

    @pl.when(step == pl.num_programs(0) - 1)
    def _():
        peak = jnp.max(pr * pr + pi * pi) + 1e-06
        scale = 0.5 / jnp.full((2 * ROWS, COLUMNS), peak, F32)
        for half, ref in enumerate((mine_ref, theirs_ref)):
            for i in range(4):
                for b in range(BLOCKS):
                    rows = pl.ds(pl.multiple_of(b * SLAB + (4 * ((place[1] + half) % 2) + i) * ROWS, ROWS), ROWS)
                    x = [jnp.concatenate([upd[part, t, rows, :] for t in range(TILES)], 1) for part in range(2)]
                    first = (b * 4 + i) * 2 * ROWS
                    ref[first : first + 2 * ROWS, :] = (jnp.concatenate(x, 0) * scale).astype(BF16)
            planes = []
            for k in range(3):
                for i in range(4):
                    first = (4 * ((place[1] + half) % 2) + i) * 4 * ROWS
                    rows = [pl.ds(pl.multiple_of(first + g * ROWS, ROWS), ROWS) for g in range(4)]
                    planes.append(jnp.concatenate([num[k, x, :] for x in rows], 1))
            ref[BLOCKS * SLAB : SUMS, :] = jnp.concatenate(planes, 0).astype(BF16)


def visit_all(place, corners, bands, probe, amplitude):
    count = amplitude.shape[0]
    fore, back = dft_blocks(FRAME)
    amp_spec = pl.BlockSpec((PER_STEP, FRAME, FRAME), lambda i: (i, 0, 0))
    return pl.pallas_call(
        visit_kernel,
        grid=(count // PER_STEP,),
        in_specs=[SMEM, SMEM] + [VMEM] * 13 + [amp_spec],
        out_specs=[VMEM] * 2,
        out_shape=[jax.ShapeDtypeStruct((SUMS, COLUMNS), BF16)] * 2,
        scratch_shapes=[
            pltpu.VMEM((2, TILES, BAND, LANES), F32),
            pltpu.VMEM((2, TILES, BAND, LANES), F32),
            pltpu.VMEM((3, FRAME, FRAME), F32),
        ],
        compiler_params=pltpu.CompilerParams(vmem_limit_bytes=48 << 20),
        cost_estimate=pl.CostEstimate(flops=count * 16 * 2 * FRAME**3, bytes_accessed=16 << 20, transcendentals=0),
    )(place, corners, *bands, probe, fore, back, amplitude)


def slab_along(value, steps):
    count = lax.axis_size("slab")
    return lax.ppermute(value, "slab", [(i, (i + steps) % count) for i in range(count)])


def x_along(value, steps):
    return lax.ppermute(value, "slab", [(i, i // 4 * 4 + (i + steps) % 4) for i in range(lax.axis_size("slab"))])


def y_along(value, steps):
    return slab_along(value, 4 * steps)


def z_along(value, steps):
    return lax.ppermute(value, "view", [(i, (i + 2 * steps) % VIEWS) for i in range(VIEWS)])


def core_swap(value):
    return lax.ppermute(value, "view", [(i, i ^ 1) for i in range(VIEWS)])


def ring_parts(along, value):
    value = lax.reduce_precision(value, exponent_bits=8, mantissa_bits=7)
    sent = value.astype(BF16)
    return [value] + [along(sent, e) for e in (1, 2, 3)]


def paired(parts):
    own, one, two, three = (x.astype(F32) for x in parts)
    return (own + two) + (one + three)


def on_device(object_field, probe, amplitude, offsets):
    layers = object_field.shape[1]
    view, slab = lax.axis_index("view"), lax.axis_index("slab")
    place = jnp.stack([view >> 1, view & 1, view * layers, slab, lax.axis_size("slab")]).astype(jnp.int32)
    corners = offsets - jnp.stack([slab * SLAB, 0]).astype(jnp.int32)

    received = core_swap(project(place, object_field, 1))
    shares = project(place, object_field, 0) + received
    piece = (shares[0] + sum(z_along(shares[e], e) for e in (1, 2, 3))).astype(BF16)
    mine = jnp.concatenate([piece] + [z_along(piece, e) for e in (1, 2, 3)], 0)
    bands = [mine] + [slab_along(mine, -k) for k in range(1, BLOCKS)]
    bands = bands + [core_swap(x) for x in bands]

    mine, theirs = visit_all(place, corners, bands, probe, amplitude)
    both = mine.astype(F32) + core_swap(theirs).astype(F32)
    update = both[:SLAB]
    for k in range(1, BLOCKS):
        term = slab_along(both[k * SLAB : (k + 1) * SLAB].astype(BF16), k).astype(F32)
        update = update + jnp.where(slab >= k, term, 0.0)
    sums = paired(ring_parts(z_along, both[BLOCKS * SLAB :]))
    update, sums = lax.optimization_barrier((update, sums))
    sent = update.astype(BF16)
    update = update + sum(z_along(sent, d).astype(F32) for d in (1, 2, 3))
    sums = paired(ring_parts(x_along, sums))
    update, sums = lax.optimization_barrier((update, sums))
    parts = ring_parts(y_along, sums)
    object_new = spread(place, update, core_swap(update), object_field)
    object_new, parts = lax.optimization_barrier((object_new, parts))
    planes = paired(parts).reshape(3, 4 * ROWS, COLUMNS)
    ratio = (planes[:2] / planes[2]).reshape(8 * ROWS, COLUMNS)
    probe_step = join(place, ratio, core_swap(ratio))
    return object_new, probe_step


def solution(mesh):
    return jax.shard_map(
        on_device,
        mesh=mesh,
        in_specs=(P(None, "view", "slab", None), P(), P(("slab", "view"), None, None), P(("slab", "view"), None)),
        out_specs=(P(None, "view", "slab", None), P()),
        check_vma=False,
    )
```

```python
import functools
import math

import jax
import jax.numpy as jnp
import ml_dtypes
import numpy as np
from jax import lax
from jax.experimental import pallas as pl
from jax.experimental.pallas import tpu as pltpu
from jax.sharding import PartitionSpec as P

F32 = jnp.float32
BF16 = jnp.bfloat16
FRAME = 256
LANES = 128
SLAB = 64
VIEWS = 8
ROWS = SLAB // VIEWS
COLUMNS = 1024
TILES = COLUMNS // LANES
BLOCKS = 5
BAND = BLOCKS * SLAB
PER_STEP = 8
SUMS = BLOCKS * SLAB + 4 * 3 * ROWS
VMEM = pl.BlockSpec(memory_space=pltpu.VMEM)
SMEM = pl.BlockSpec(memory_space=pltpu.SMEM)


def dft_blocks(order):
    index = np.arange(order, dtype=np.int32)
    product = index[:, None] * index[None, :] % order
    angle = product.astype(np.float32) * np.float32(-2.0 * math.pi / order)
    factor = np.float32(1.0 / math.sqrt(order))
    c, s = np.cos(angle) * factor, np.sin(angle) * factor
    fore = np.block([[c, -s], [s, c]]).astype(ml_dtypes.bfloat16)
    back = np.block([[c, s], [-s, c]]).astype(ml_dtypes.bfloat16)
    return fore, back


def tiles_of(value):
    return [value[:, t * LANES : (t + 1) * LANES] for t in range(TILES)]


def to_right(tiles, steps):
    lane = lax.broadcasted_iota(jnp.int32, tiles[0].shape, 1)
    turned = [pltpu.roll(x, steps, 1) for x in tiles]
    return [jnp.where(lane >= steps, x, before) for x, before in zip(turned, [jnp.zeros_like(tiles[0])] + turned)]


def to_left(tiles, steps):
    lane = lax.broadcasted_iota(jnp.int32, tiles[0].shape, 1)
    turned = [pltpu.roll(x, (LANES - steps) % LANES, 1) for x in tiles]
    return [jnp.where(lane < LANES - steps, x, after) for x, after in zip(turned, turned[1:] + [jnp.zeros_like(tiles[0])])]


def chunk_at(place, half, e):
    return 4 * ((place[1] + half) % 2) + (place[0] + e) % 4


def rows_at(place, half, i):
    return pl.ds(pl.multiple_of((4 * ((place[1] + half) % 2) + i) * ROWS, ROWS), ROWS)


def project_kernel(half, place, field_ref, out_ref, held, sems):
    layers = field_ref.shape[1]
    copies = []
    for e in range(4):
        rows = pl.ds(pl.multiple_of(chunk_at(place, half, e) * ROWS, ROWS), ROWS)
        copies.append(pltpu.make_async_copy(field_ref.at[:, :, rows, :], held.at[e], sems.at[e]))
        copies[-1].start()
    for e in range(4):
        copies[e].wait()
        values = [tiles_of(jnp.concatenate([held[e, 0, k], held[e, 1, k]], 0)) for k in range(layers)]
        steps = 1
        while len(values) > 1:
            moved = [to_right(x, steps) for x in values[1::2]]
            values = [[a + b for a, b in zip(x, y)] for x, y in zip(values[0::2], moved)]
            steps *= 2
        for t, x in enumerate(to_right(values[0], place[2])):
            out_ref[e, :, t * LANES : (t + 1) * LANES] = x


def project(place, field, half):
    layers = field.shape[1]
    return pl.pallas_call(
        functools.partial(project_kernel, half),
        in_specs=[SMEM, pl.BlockSpec(memory_space=pl.ANY)],
        out_specs=VMEM,
        out_shape=jax.ShapeDtypeStruct((4, 2 * ROWS, COLUMNS), F32),
        scratch_shapes=[pltpu.VMEM((4, 2, layers, ROWS, COLUMNS), F32), pltpu.SemaphoreType.DMA((4,))],
        compiler_params=pltpu.CompilerParams(vmem_limit_bytes=60 << 20),
        cost_estimate=pl.CostEstimate(flops=layers * 4 * 16 * 1024 * 6, bytes_accessed=12 << 20, transcendentals=0),
    )(place, field)


def spread_kernel(place, mine_ref, theirs_ref, field_ref, out_ref, held, sems):
    layers = field_ref.shape[1]
    copies = []
    for half, ref in enumerate((mine_ref, theirs_ref)):
        for i in range(4):
            rows, slot = rows_at(place, half, i), half * 4 + i
            base = to_left(tiles_of(ref[i * 2 * ROWS : (i + 1) * 2 * ROWS, :].astype(F32)), place[2])
            for k in range(layers):
                for t, x in enumerate(to_left(base, k) if k else base):
                    columns = slice(t * LANES, (t + 1) * LANES)
                    for part in range(2):
                        held[slot, part, k, :, columns] = field_ref[part, k, rows, columns] + x[part * ROWS : (part + 1) * ROWS]
            copies.append(pltpu.make_async_copy(held.at[slot], out_ref.at[:, :, rows, :], sems.at[slot]))
            copies[-1].start()
    for copy in copies:
        copy.wait()


def spread(place, mine, theirs, field):
    layers = field.shape[1]
    return pl.pallas_call(
        spread_kernel,
        in_specs=[SMEM, VMEM, VMEM, VMEM],
        out_specs=pl.BlockSpec(memory_space=pl.ANY),
        out_shape=jax.ShapeDtypeStruct(field.shape, F32),
        scratch_shapes=[pltpu.VMEM((VIEWS, 2, layers, ROWS, COLUMNS), F32), pltpu.SemaphoreType.DMA((VIEWS,))],
        compiler_params=pltpu.CompilerParams(vmem_limit_bytes=20 << 20),
        cost_estimate=pl.CostEstimate(flops=layers * 8 * 16 * 1024 * 4, bytes_accessed=16 << 20, transcendentals=0),
    )(place, mine, theirs, field)


def join_kernel(place, mine_ref, theirs_ref, out_ref):
    for half, ref in enumerate((mine_ref, theirs_ref)):
        for part in range(2):
            for i in range(4):
                x = ref[(part * 4 + i) * ROWS : (part * 4 + i + 1) * ROWS, :]
                for g in range(4):
                    start = ((4 * ((place[1] + half) % 2) + i) * 4 + g) * ROWS
                    out_ref[part, pl.ds(pl.multiple_of(start, ROWS), ROWS), :] = x[:, g * FRAME : (g + 1) * FRAME]


def join(place, mine, theirs):
    return pl.pallas_call(
        join_kernel,
        in_specs=[SMEM, VMEM, VMEM],
        out_specs=VMEM,
        out_shape=jax.ShapeDtypeStruct((2, FRAME, FRAME), F32),
        compiler_params=pltpu.CompilerParams(vmem_limit_bytes=8 << 20),
        cost_estimate=pl.CostEstimate(flops=1000, bytes_accessed=1 << 20, transcendentals=0),
    )(place, mine, theirs)


def dot(left, right):
    return jnp.dot(left, right, preferred_element_type=F32)


def visit_kernel(place, off_ref, *refs):
    bands, (probe_ref, fore_ref, back_ref, amp_ref, mine_ref, theirs_ref, band, upd, num) = refs[: 2 * BLOCKS], refs[2 * BLOCKS :]
    step = pl.program_id(0)

    @pl.when(step == 0)
    def _():
        for i, ref in enumerate(bands):
            half, block = divmod(i, BLOCKS)
            for j in range(4):
                x = ref[j * 2 * ROWS : (j + 1) * 2 * ROWS, :].astype(F32)
                x = jnp.where(place[3] + block < place[4], x, 0.0)
                first = pl.multiple_of(block * SLAB + chunk_at(place, half, 4 - j) * ROWS, ROWS)
                for part in range(2):
                    for t in range(TILES):
                        band[part, t, pl.ds(first, ROWS), :] = x[part * ROWS : (part + 1) * ROWS, t * LANES : (t + 1) * LANES]
        upd[...] = jnp.zeros_like(upd)
        num[...] = jnp.zeros_like(num)

    lane = lax.broadcasted_iota(jnp.int32, (FRAME, LANES), 1)

    def corner(j):
        p = step * PER_STEP + j
        r, c = off_ref[p, 0], off_ref[p, 1]
        q, m = c // LANES, c % LANES
        return r, (q, q + 1, jnp.minimum(q + 2, TILES - 1)), m

    def patch_of(part, r, q, m):
        turn = (LANES - m) % LANES
        tiles = [pltpu.roll(band[part, t, pl.ds(r, FRAME), :], turn, 1) for t in q]
        keep = lane < LANES - m
        return jnp.concatenate([jnp.where(keep, tiles[0], tiles[1]), jnp.where(keep, tiles[1], tiles[2])], 1)

    def add_to(part, value, r, q, m):
        left = pltpu.roll(value[:, :LANES], m, 1)
        right = pltpu.roll(value[:, LANES:], m, 1)
        keep = lane >= m
        terms = [jnp.where(keep, left, 0.0), jnp.where(keep, right, left), jnp.where(keep, 0.0, right)]
        for t, x in zip(q, terms):
            upd[part, t, pl.ds(r, FRAME), :] += x

    pr, pi = probe_ref[0], probe_ref[1]
    corners = [corner(j) for j in range(PER_STEP)]
    kept = [dict() for _ in range(PER_STEP)]

    def enter(j, at):
        r, q, m = corners[j]
        at["a"], at["b"] = a, b = patch_of(0, r, q, m), patch_of(1, r, q, m)
        at["er"], at["ei"] = pr * a - pi * b, pr * b + pi * a

    def rows_out(j, at):
        h = dot(fore_ref[...], jnp.concatenate([at["er"], at["ei"]], 0).astype(BF16))
        at["half"] = jnp.concatenate([h[:FRAME], h[FRAME:]], 1).astype(BF16)

    def columns_out(j, at):
        at["far"] = dot(at["half"], back_ref[...])

    def fix(j, at):
        fr, fi = at["far"][:, :FRAME], at["far"][:, FRAME:]
        factor = amp_ref[j] * lax.rsqrt(fr * fr + fi * fi + 0.25)
        at["fixed"] = jnp.concatenate([fr * factor, fi * factor], 1).astype(BF16)

    def columns_back(j, at):
        h = dot(at["fixed"], fore_ref[...])
        at["back"] = jnp.concatenate([h[:, :FRAME], h[:, FRAME:]], 0).astype(BF16)

    def rows_back(j, at):
        at["new"] = dot(back_ref[...], at["back"])

    def leave(j, at):
        a, b = at["a"], at["b"]
        dr, di = at["new"][:FRAME] - at["er"], at["new"][FRAME:] - at["ei"]
        r, q, m = corners[j]
        add_to(0, pr * dr + pi * di, r, q, m)
        add_to(1, pr * di - pi * dr, r, q, m)
        num[0] += a * dr + b * di
        num[1] += a * di - b * dr
        num[2] += a * a + b * b

    stages = (enter, rows_out, columns_out, fix, columns_back, rows_back, leave)
    for tick in range(2 * (PER_STEP - 1) + len(stages)):
        due = [(tick - 2 * j, j) for j in range(PER_STEP) if 0 <= tick - 2 * j < len(stages)]
        for k, j in due:
            stages[k](j, kept[j])

    @pl.when(step == pl.num_programs(0) - 1)
    def _():
        peak = jnp.max(pr * pr + pi * pi) + 1e-06
        scale = 0.5 / jnp.full((2 * ROWS, COLUMNS), peak, F32)
        for half, ref in enumerate((mine_ref, theirs_ref)):
            for i in range(4):
                for b in range(BLOCKS):
                    rows = pl.ds(pl.multiple_of(b * SLAB + (4 * ((place[1] + half) % 2) + i) * ROWS, ROWS), ROWS)
                    x = [jnp.concatenate([upd[part, t, rows, :] for t in range(TILES)], 1) for part in range(2)]
                    first = (b * 4 + i) * 2 * ROWS
                    ref[first : first + 2 * ROWS, :] = (jnp.concatenate(x, 0) * scale).astype(BF16)
            planes = []
            for k in range(3):
                for i in range(4):
                    first = (4 * ((place[1] + half) % 2) + i) * 4 * ROWS
                    rows = [pl.ds(pl.multiple_of(first + g * ROWS, ROWS), ROWS) for g in range(4)]
                    planes.append(jnp.concatenate([num[k, x, :] for x in rows], 1))
            ref[BLOCKS * SLAB : SUMS, :] = jnp.concatenate(planes, 0).astype(BF16)


def visit_all(place, corners, bands, probe, amplitude):
    count = amplitude.shape[0]
    fore, back = dft_blocks(FRAME)
    amp_spec = pl.BlockSpec((PER_STEP, FRAME, FRAME), lambda i: (i, 0, 0))
    return pl.pallas_call(
        visit_kernel,
        grid=(count // PER_STEP,),
        in_specs=[SMEM, SMEM] + [VMEM] * 13 + [amp_spec],
        out_specs=[VMEM] * 2,
        out_shape=[jax.ShapeDtypeStruct((SUMS, COLUMNS), BF16)] * 2,
        scratch_shapes=[
            pltpu.VMEM((2, TILES, BAND, LANES), F32),
            pltpu.VMEM((2, TILES, BAND, LANES), F32),
            pltpu.VMEM((3, FRAME, FRAME), F32),
        ],
        compiler_params=pltpu.CompilerParams(vmem_limit_bytes=46 << 20),
        cost_estimate=pl.CostEstimate(flops=count * 16 * 2 * FRAME**3, bytes_accessed=16 << 20, transcendentals=0),
    )(place, corners, *bands, probe, fore, back, amplitude)


def slab_along(value, steps):
    count = lax.axis_size("slab")
    return lax.ppermute(value, "slab", [(i, (i + steps) % count) for i in range(count)])


def x_along(value, steps):
    return lax.ppermute(value, "slab", [(i, i // 4 * 4 + (i + steps) % 4) for i in range(lax.axis_size("slab"))])


def y_along(value, steps):
    return slab_along(value, 4 * steps)


def z_along(value, steps):
    return lax.ppermute(value, "view", [(i, (i + 2 * steps) % VIEWS) for i in range(VIEWS)])


def core_swap(value):
    return lax.ppermute(value, "view", [(i, i ^ 1) for i in range(VIEWS)])


def ring_parts(along, value):
    value = lax.reduce_precision(value, exponent_bits=8, mantissa_bits=7)
    sent = value.astype(BF16)
    return [value] + [along(sent, e) for e in (1, 2, 3)]


def paired(parts):
    own, one, two, three = (x.astype(F32) for x in parts)
    return (own + two) + (one + three)


def on_device(object_field, probe, amplitude, offsets):
    layers = object_field.shape[1]
    view, slab = lax.axis_index("view"), lax.axis_index("slab")
    place = jnp.stack([view >> 1, view & 1, view * layers, slab, lax.axis_size("slab")]).astype(jnp.int32)
    corners = offsets - jnp.stack([slab * SLAB, 0]).astype(jnp.int32)

    received = core_swap(project(place, object_field, 1))
    shares = project(place, object_field, 0) + received
    piece = (shares[0] + sum(z_along(shares[e], e) for e in (1, 2, 3))).astype(BF16)
    mine = jnp.concatenate([piece] + [z_along(piece, e) for e in (1, 2, 3)], 0)
    bands = [mine] + [slab_along(mine, -k) for k in range(1, BLOCKS)]
    bands = bands + [core_swap(x) for x in bands]

    mine, theirs = visit_all(place, corners, bands, probe, amplitude)
    both = mine.astype(F32) + core_swap(theirs).astype(F32)
    parts = ring_parts(z_along, both[BLOCKS * SLAB :])
    update = both[:SLAB]
    for k in range(1, BLOCKS):
        term = slab_along(both[k * SLAB : (k + 1) * SLAB].astype(BF16), k).astype(F32)
        update = update + jnp.where(slab >= k, term, 0.0)
    sums = paired(parts)
    update, sums = lax.optimization_barrier((update, sums))
    sent = update.astype(BF16)
    update = update + sum(z_along(sent, d).astype(F32) for d in (1, 2, 3))
    sums = paired(ring_parts(x_along, sums))
    update, sums = lax.optimization_barrier((update, sums))
    parts = ring_parts(y_along, sums)
    object_new = spread(place, update, core_swap(update), object_field)
    object_new, parts = lax.optimization_barrier((object_new, parts))
    planes = paired(parts).reshape(3, 4 * ROWS, COLUMNS)
    ratio = (planes[:2] / planes[2]).reshape(8 * ROWS, COLUMNS)
    probe_step = join(place, ratio, core_swap(ratio))
    return object_new, probe_step


def solution(mesh):
    return jax.shard_map(
        on_device,
        mesh=mesh,
        in_specs=(P(None, "view", "slab", None), P(), P(("slab", "view"), None, None), P(("slab", "view"), None)),
        out_specs=(P(None, "view", "slab", None), P()),
        check_vma=False,
    )
```

```python
import functools
import math

import jax
import jax.numpy as jnp
import ml_dtypes
import numpy as np
from jax import lax
from jax.experimental import pallas as pl
from jax.experimental.pallas import tpu as pltpu
from jax.sharding import PartitionSpec as P

F32 = jnp.float32
BF16 = jnp.bfloat16
FRAME = 256
LANES = 128
SLAB = 64
VIEWS = 8
ROWS = SLAB // VIEWS
COLUMNS = 1024
TILES = COLUMNS // LANES
BLOCKS = 5
BAND = BLOCKS * SLAB
PER_STEP = 8
SUMS = BLOCKS * SLAB + 4 * 3 * ROWS
VMEM = pl.BlockSpec(memory_space=pltpu.VMEM)
SMEM = pl.BlockSpec(memory_space=pltpu.SMEM)


def dft_blocks(order):
    index = np.arange(order, dtype=np.int32)
    product = index[:, None] * index[None, :] % order
    angle = product.astype(np.float32) * np.float32(-2.0 * math.pi / order)
    factor = np.float32(1.0 / math.sqrt(order))
    c, s = np.cos(angle) * factor, np.sin(angle) * factor
    fore = np.block([[c, -s], [s, c]]).astype(ml_dtypes.bfloat16)
    back = np.block([[c, s], [-s, c]]).astype(ml_dtypes.bfloat16)
    return fore, back


def tiles_of(value):
    return [value[:, t * LANES : (t + 1) * LANES] for t in range(TILES)]


def to_right(tiles, steps):
    lane = lax.broadcasted_iota(jnp.int32, tiles[0].shape, 1)
    turned = [pltpu.roll(x, steps, 1) for x in tiles]
    return [jnp.where(lane >= steps, x, before) for x, before in zip(turned, [jnp.zeros_like(tiles[0])] + turned)]


def to_left(tiles, steps):
    lane = lax.broadcasted_iota(jnp.int32, tiles[0].shape, 1)
    turned = [pltpu.roll(x, (LANES - steps) % LANES, 1) for x in tiles]
    return [jnp.where(lane < LANES - steps, x, after) for x, after in zip(turned, turned[1:] + [jnp.zeros_like(tiles[0])])]


def chunk_at(place, half, e):
    return 4 * ((place[1] + half) % 2) + (place[0] + e) % 4


def rows_at(place, half, i):
    return pl.ds(pl.multiple_of((4 * ((place[1] + half) % 2) + i) * ROWS, ROWS), ROWS)


def project_kernel(half, place, field_ref, out_ref, held, sems):
    layers = field_ref.shape[1]
    copies = []
    for e in range(4):
        rows = pl.ds(pl.multiple_of(chunk_at(place, half, e) * ROWS, ROWS), ROWS)
        copies.append(pltpu.make_async_copy(field_ref.at[:, :, rows, :], held.at[e], sems.at[e]))
        copies[-1].start()
    for e in range(4):
        copies[e].wait()
        values = [tiles_of(jnp.concatenate([held[e, 0, k], held[e, 1, k]], 0)) for k in range(layers)]
        steps = 1
        while len(values) > 1:
            moved = [to_right(x, steps) for x in values[1::2]]
            values = [[a + b for a, b in zip(x, y)] for x, y in zip(values[0::2], moved)]
            steps *= 2
        for t, x in enumerate(to_right(values[0], place[2])):
            out_ref[e, :, t * LANES : (t + 1) * LANES] = x


def project(place, field, half):
    layers = field.shape[1]
    return pl.pallas_call(
        functools.partial(project_kernel, half),
        in_specs=[SMEM, pl.BlockSpec(memory_space=pl.ANY)],
        out_specs=VMEM,
        out_shape=jax.ShapeDtypeStruct((4, 2 * ROWS, COLUMNS), F32),
        scratch_shapes=[pltpu.VMEM((4, 2, layers, ROWS, COLUMNS), F32), pltpu.SemaphoreType.DMA((4,))],
        compiler_params=pltpu.CompilerParams(vmem_limit_bytes=60 << 20),
        cost_estimate=pl.CostEstimate(flops=layers * 4 * 16 * 1024 * 6, bytes_accessed=12 << 20, transcendentals=0),
    )(place, field)


def spread_kernel(place, mine_ref, theirs_ref, field_ref, out_ref, held, sems):
    layers = field_ref.shape[1]
    copies = []
    for half, ref in enumerate((mine_ref, theirs_ref)):
        for i in range(4):
            rows, slot = rows_at(place, half, i), half * 4 + i
            base = to_left(tiles_of(ref[i * 2 * ROWS : (i + 1) * 2 * ROWS, :].astype(F32)), place[2])
            for k in range(layers):
                for t, x in enumerate(to_left(base, k) if k else base):
                    columns = slice(t * LANES, (t + 1) * LANES)
                    for part in range(2):
                        held[slot, part, k, :, columns] = field_ref[part, k, rows, columns] + x[part * ROWS : (part + 1) * ROWS]
            copies.append(pltpu.make_async_copy(held.at[slot], out_ref.at[:, :, rows, :], sems.at[slot]))
            copies[-1].start()
    for copy in copies:
        copy.wait()


def spread(place, mine, theirs, field):
    layers = field.shape[1]
    return pl.pallas_call(
        spread_kernel,
        in_specs=[SMEM, VMEM, VMEM, VMEM],
        out_specs=pl.BlockSpec(memory_space=pl.ANY),
        out_shape=jax.ShapeDtypeStruct(field.shape, F32),
        scratch_shapes=[pltpu.VMEM((VIEWS, 2, layers, ROWS, COLUMNS), F32), pltpu.SemaphoreType.DMA((VIEWS,))],
        compiler_params=pltpu.CompilerParams(vmem_limit_bytes=20 << 20),
        cost_estimate=pl.CostEstimate(flops=layers * 8 * 16 * 1024 * 4, bytes_accessed=16 << 20, transcendentals=0),
    )(place, mine, theirs, field)


def join_kernel(place, mine_ref, theirs_ref, out_ref):
    for half, ref in enumerate((mine_ref, theirs_ref)):
        for part in range(2):
            for i in range(4):
                x = ref[(part * 4 + i) * ROWS : (part * 4 + i + 1) * ROWS, :]
                for g in range(4):
                    start = ((4 * ((place[1] + half) % 2) + i) * 4 + g) * ROWS
                    out_ref[part, pl.ds(pl.multiple_of(start, ROWS), ROWS), :] = x[:, g * FRAME : (g + 1) * FRAME]


def join(place, mine, theirs):
    return pl.pallas_call(
        join_kernel,
        in_specs=[SMEM, VMEM, VMEM],
        out_specs=VMEM,
        out_shape=jax.ShapeDtypeStruct((2, FRAME, FRAME), F32),
        compiler_params=pltpu.CompilerParams(vmem_limit_bytes=8 << 20),
        cost_estimate=pl.CostEstimate(flops=1000, bytes_accessed=1 << 20, transcendentals=0),
    )(place, mine, theirs)


def dot(left, right):
    return jnp.dot(left, right, preferred_element_type=F32)


def visit_kernel(place, off_ref, *refs):
    bands, (probe_ref, fore_ref, back_ref, amp_ref, mine_ref, theirs_ref, band, upd, num) = refs[: 2 * BLOCKS], refs[2 * BLOCKS :]
    step = pl.program_id(0)

    @pl.when(step == 0)
    def _():
        for i, ref in enumerate(bands):
            half, block = divmod(i, BLOCKS)
            for j in range(4):
                x = ref[j * 2 * ROWS : (j + 1) * 2 * ROWS, :].astype(F32)
                x = jnp.where(place[3] + block < place[4], x, 0.0)
                first = pl.multiple_of(block * SLAB + chunk_at(place, half, 4 - j) * ROWS, ROWS)
                for part in range(2):
                    for t in range(TILES):
                        band[part, t, pl.ds(first, ROWS), :] = x[part * ROWS : (part + 1) * ROWS, t * LANES : (t + 1) * LANES]
        upd[...] = jnp.zeros_like(upd)
        num[...] = jnp.zeros_like(num)

    lane = lax.broadcasted_iota(jnp.int32, (FRAME, LANES), 1)

    def corner(j):
        p = step * PER_STEP + j
        r, c = off_ref[p, 0], off_ref[p, 1]
        q, m = c // LANES, c % LANES
        return r, (q, q + 1, jnp.minimum(q + 2, TILES - 1)), m

    def patch_of(part, r, q, m):
        turn = (LANES - m) % LANES
        tiles = [pltpu.roll(band[part, t, pl.ds(r, FRAME), :], turn, 1) for t in q]
        keep = lane < LANES - m
        return jnp.concatenate([jnp.where(keep, tiles[0], tiles[1]), jnp.where(keep, tiles[1], tiles[2])], 1)

    def add_to(part, value, r, q, m):
        left = pltpu.roll(value[:, :LANES], m, 1)
        right = pltpu.roll(value[:, LANES:], m, 1)
        keep = lane >= m
        terms = [jnp.where(keep, left, 0.0), jnp.where(keep, right, left), jnp.where(keep, 0.0, right)]
        for t, x in zip(q, terms):
            upd[part, t, pl.ds(r, FRAME), :] += x

    pr, pi = probe_ref[0], probe_ref[1]
    corners = [corner(j) for j in range(PER_STEP)]
    kept = [dict() for _ in range(PER_STEP)]

    def enter(j, at):
        r, q, m = corners[j]
        at["a"], at["b"] = a, b = patch_of(0, r, q, m), patch_of(1, r, q, m)
        at["er"], at["ei"] = pr * a - pi * b, pr * b + pi * a

    def rows_out(j, at):
        h = dot(fore_ref[...], jnp.concatenate([at["er"], at["ei"]], 0).astype(BF16))
        at["half"] = jnp.concatenate([h[:FRAME], h[FRAME:]], 1).astype(BF16)

    def columns_out(j, at):
        at["far"] = dot(at["half"], back_ref[...])

    def fix(j, at):
        fr, fi = at["far"][:, :FRAME], at["far"][:, FRAME:]
        factor = amp_ref[j] * lax.rsqrt(fr * fr + fi * fi + 0.25)
        at["fixed"] = jnp.concatenate([fr * factor, fi * factor], 1).astype(BF16)

    def columns_back(j, at):
        h = dot(at["fixed"], fore_ref[...])
        at["back"] = jnp.concatenate([h[:, :FRAME], h[:, FRAME:]], 0).astype(BF16)

    def rows_back(j, at):
        at["new"] = dot(back_ref[...], at["back"])

    def leave(j, at):
        a, b = at["a"], at["b"]
        dr, di = at["new"][:FRAME] - at["er"], at["new"][FRAME:] - at["ei"]
        r, q, m = corners[j]
        add_to(0, pr * dr + pi * di, r, q, m)
        add_to(1, pr * di - pi * dr, r, q, m)
        num[0] += a * dr + b * di
        num[1] += a * di - b * dr
        num[2] += a * a + b * b

    stages = (enter, rows_out, columns_out, fix, columns_back, rows_back, leave)
    for tick in range(2 * (PER_STEP - 1) + len(stages)):
        due = [(tick - 2 * j, j) for j in range(PER_STEP) if 0 <= tick - 2 * j < len(stages)]
        for k, j in due:
            stages[k](j, kept[j])

    @pl.when(step == pl.num_programs(0) - 1)
    def _():
        peak = jnp.max(pr * pr + pi * pi) + 1e-06
        scale = 0.5 / jnp.full((2 * ROWS, COLUMNS), peak, F32)
        for half, ref in enumerate((mine_ref, theirs_ref)):
            for i in range(4):
                for b in range(BLOCKS):
                    rows = pl.ds(pl.multiple_of(b * SLAB + (4 * ((place[1] + half) % 2) + i) * ROWS, ROWS), ROWS)
                    x = [jnp.concatenate([upd[part, t, rows, :] for t in range(TILES)], 1) for part in range(2)]
                    first = (b * 4 + i) * 2 * ROWS
                    ref[first : first + 2 * ROWS, :] = (jnp.concatenate(x, 0) * scale).astype(BF16)
            planes = []
            for k in range(3):
                for i in range(4):
                    first = (4 * ((place[1] + half) % 2) + i) * 4 * ROWS
                    rows = [pl.ds(pl.multiple_of(first + g * ROWS, ROWS), ROWS) for g in range(4)]
                    planes.append(jnp.concatenate([num[k, x, :] for x in rows], 1))
            ref[BLOCKS * SLAB : SUMS, :] = jnp.concatenate(planes, 0).astype(BF16)


def visit_all(place, corners, bands, probe, amplitude):
    count = amplitude.shape[0]
    fore, back = dft_blocks(FRAME)
    amp_spec = pl.BlockSpec((PER_STEP, FRAME, FRAME), lambda i: (i, 0, 0))
    return pl.pallas_call(
        visit_kernel,
        grid=(count // PER_STEP,),
        in_specs=[SMEM, SMEM] + [VMEM] * 13 + [amp_spec],
        out_specs=[VMEM] * 2,
        out_shape=[jax.ShapeDtypeStruct((SUMS, COLUMNS), BF16)] * 2,
        scratch_shapes=[
            pltpu.VMEM((2, TILES, BAND, LANES), F32),
            pltpu.VMEM((2, TILES, BAND, LANES), F32),
            pltpu.VMEM((3, FRAME, FRAME), F32),
        ],
        compiler_params=pltpu.CompilerParams(vmem_limit_bytes=44 << 20),
        cost_estimate=pl.CostEstimate(flops=count * 16 * 2 * FRAME**3, bytes_accessed=16 << 20, transcendentals=0),
    )(place, corners, *bands, probe, fore, back, amplitude)


def slab_along(value, steps):
    count = lax.axis_size("slab")
    return lax.ppermute(value, "slab", [(i, (i + steps) % count) for i in range(count)])


def x_along(value, steps):
    return lax.ppermute(value, "slab", [(i, i // 4 * 4 + (i + steps) % 4) for i in range(lax.axis_size("slab"))])


def y_along(value, steps):
    return slab_along(value, 4 * steps)


def z_along(value, steps):
    return lax.ppermute(value, "view", [(i, (i + 2 * steps) % VIEWS) for i in range(VIEWS)])


def core_swap(value):
    return lax.ppermute(value, "view", [(i, i ^ 1) for i in range(VIEWS)])


def ring_parts(along, value):
    value = lax.reduce_precision(value, exponent_bits=8, mantissa_bits=7)
    sent = value.astype(BF16)
    return [value] + [along(sent, e) for e in (1, 2, 3)]


def paired(parts):
    own, one, two, three = (x.astype(F32) for x in parts)
    return (own + two) + (one + three)


def on_device(object_field, probe, amplitude, offsets):
    layers = object_field.shape[1]
    view, slab = lax.axis_index("view"), lax.axis_index("slab")
    place = jnp.stack([view >> 1, view & 1, view * layers, slab, lax.axis_size("slab")]).astype(jnp.int32)
    corners = offsets - jnp.stack([slab * SLAB, 0]).astype(jnp.int32)

    received = core_swap(project(place, object_field, 1))
    shares = project(place, object_field, 0) + received
    piece = (shares[0] + sum(z_along(shares[e], e) for e in (1, 2, 3))).astype(BF16)
    mine = jnp.concatenate([piece] + [z_along(piece, e) for e in (1, 2, 3)], 0)
    bands = [mine] + [slab_along(mine, -k) for k in range(1, BLOCKS)]
    bands = bands + [core_swap(x) for x in bands]

    mine, theirs = visit_all(place, corners, bands, probe, amplitude)
    both = mine.astype(F32) + core_swap(theirs).astype(F32)
    parts = ring_parts(z_along, both[BLOCKS * SLAB :])
    update = both[:SLAB]
    for k in range(1, BLOCKS):
        term = slab_along(both[k * SLAB : (k + 1) * SLAB].astype(BF16), k).astype(F32)
        update = update + jnp.where(slab >= k, term, 0.0)
    sums = paired(parts)
    update, sums = lax.optimization_barrier((update, sums))
    sent = update.astype(BF16)
    update = update + sum(z_along(sent, d).astype(F32) for d in (1, 2, 3))
    sums = paired(ring_parts(x_along, sums))
    update, sums = lax.optimization_barrier((update, sums))
    parts = ring_parts(y_along, sums)
    object_new = spread(place, update, core_swap(update), object_field)
    object_new, parts = lax.optimization_barrier((object_new, parts))
    planes = paired(parts).reshape(3, 4 * ROWS, COLUMNS)
    ratio = (planes[:2] / planes[2]).reshape(8 * ROWS, COLUMNS)
    probe_step = join(place, ratio, core_swap(ratio))
    return object_new, probe_step


def solution(mesh):
    return jax.shard_map(
        on_device,
        mesh=mesh,
        in_specs=(P(None, "view", "slab", None), P(), P(("slab", "view"), None, None), P(("slab", "view"), None)),
        out_specs=(P(None, "view", "slab", None), P()),
        check_vma=False,
    )
```
